32 devices in a mesh: dp: 4 (over z), fsdp: 4 (over y, x), tensor: 2 (over core).
Axes of the slice: x: 2, y: 2, z: 4, core: 2. Of those that a mesh axis runs over, the one named last changes fastest.
Arguments:
- activations: bfloat16 [4096, 8192], P(('dp', 'fsdp')), may hold values from -6 to 6
- out_grads: bfloat16 [4096, 2, 2048], P(('dp', 'fsdp'), 'tensor'), may hold values from -0.09375 to 0.09375
- basis: bfloat16 [8192, 1024], P('dp'), may hold values from -0.0625 to 0.0625
- weights: bfloat16 [2, 2048, 8192], P('tensor', ('dp', 'fsdp')), may hold values from -3 to 3
- first_moment: float32 [2, 2048, 1024], P('tensor', ('dp', 'fsdp')), may hold values from -2 to 2
- second_moment: float32 [2, 2048, 1024], P('tensor', ('dp', 'fsdp')), may hold values from 0.0001 to 0.01
Outputs:
- new_weights: bfloat16 [2, 2048, 8192], P('tensor', 'dp')
- first_new: float32 [2, 2048, 1024], P('tensor', ('dp', 'fsdp'))
- second_new: float32 [2, 2048, 1024], P('tensor', ('dp', 'fsdp'))
The draws below stay inside these ranges and needn't reach their ends.
All inputs are finite; a program needn't handle non-finite values.
Results may differ from the reference program's by a relative error of at most 0.012.
Values may be sent and summed in bfloat16 or wider, within the bound.
A program may use at most 128 MiB of HBM per device.

```python
import math
import jax
import jax.numpy as jnp

D = 8192
RANK = 1024
STEP = 10
GROUPS = 2
HALF = 2048
TOKENS = 4096


def levels(stream_key, dims, split, low, high):
    def one(dim, blocks):
        heights = jax.random.uniform(jax.random.fold_in(jax.random.fold_in(stream_key, 6), dim), (blocks,), jnp.float32, low / len(split), high / len(split))
        return jnp.repeat(jnp.exp(heights), dims[dim] // blocks).reshape((-1,) + (1,) * (len(dims) - dim - 1))

    loudness = one(*split[0])
    for cut in split[1:]:
        loudness = loudness * one(*cut)
    return loudness


def centred(own_key, extent, deviation, most, cuts=(), dtype=jnp.bfloat16):
    array = deviation * jax.random.normal(own_key, extent, jnp.float32)
    if cuts:
        array = array * levels(own_key, extent, cuts, -0.22, 0.18)
    return jnp.clip(array, -most, most).astype(dtype)


def setup_inputs(seed: int = 0) -> dict:
    streams_of = jax.random.split(jax.random.key(seed), 7)
    activations = centred(streams_of[0], (TOKENS, D), 1.0, 6.0, ((0, 16),))
    out_grads = centred(streams_of[1], (TOKENS, GROUPS, HALF), (1.0 / TOKENS ** 0.5), 0.09375, ((0, 16), (1, 2)))
    basis = centred(streams_of[2], (D, RANK), D ** -0.5, 0.0625, ((0, 4),))
    weights = centred(streams_of[3], (GROUPS, HALF, D), 0.5, 3.0, ((0, 2), (1, 16)))
    first_moment = centred(streams_of[4], (GROUPS, HALF, RANK), 0.3, 2.0, ((0, 2), (1, 16)), jnp.float32)
    second_moment = jnp.clip(jnp.exp(math.log(0.01) - 4.6051702 * jax.random.uniform(streams_of[5], (GROUPS, HALF, RANK), jnp.float32) ** levels(streams_of[5], (GROUPS, HALF, RANK), ((0, 2), (1, 16)), -0.2, 0.2)), 0.0001, 0.01)
    return dict(activations=activations, out_grads=out_grads, basis=basis, weights=weights, first_moment=first_moment, second_moment=second_moment)


beta_one = 0.9
beta_two = 0.999
epsilon = 1e-08
step_scale = 0.25

def reference(activations, out_grads, basis, weights, first_moment, second_moment):
    low_rank = jnp.dot(activations, basis, preferred_element_type=jnp.float32).astype(jnp.bfloat16)
    cotangent = out_grads.reshape(TOKENS, GROUPS * HALF)
    projected = jnp.dot(cotangent.T, low_rank, preferred_element_type=jnp.float32)
    projected = projected.reshape(GROUPS, HALF, RANK)
    first_new = beta_one * first_moment + (1.0 - beta_one) * projected
    second_new = beta_two * second_moment + (1.0 - beta_two) * projected * projected
    corrected = first_new / (1.0 - beta_one ** STEP)
    scaled = jnp.sqrt(second_new / (1.0 - beta_two ** STEP)) + epsilon
    direction = (corrected / scaled).astype(jnp.bfloat16)
    update = jnp.dot(direction.reshape(GROUPS * HALF, RANK), basis.T, preferred_element_type=jnp.float32)
    update = update.reshape(GROUPS, HALF, D)
    new_weights = (weights.astype(jnp.float32) - step_scale * update).astype(jnp.bfloat16)
    return (new_weights, first_new, second_new)
```

```python
import functools

import jax
import jax.numpy as jnp
from jax import lax
from jax.experimental import pallas as pl
from jax.experimental.pallas import tpu as pltpu
from jax.sharding import PartitionSpec as P

STEP = 10
MESH = pl.DeviceIdType.MESH
F32 = jnp.float32
BF16 = jnp.bfloat16

beta_one = 0.9
beta_two = 0.999
epsilon = 1e-08
step_scale = 0.25

FROM_Z, FROM_A, FROM_B, HALF0_B, HALF1_A, SIB_OWN, SIB_A, SIB_B, SIB_H0, SIB_H1 = range(10)


def kernel(
    nz, act_ref, grads_ref, basis_ref, weights_ref, first_ref, second_ref,
    basis_out, weights_out, direction_out, first_out, second_out,
    act, basis, grads, low, part_out, part_in, part_own, direction, acc,
    local, send, arrive_basis, arrive_grads, arrive_low, arrive_part, arrive_dir, arrive_w,
):
    z, j, c = lax.axis_index("dp"), lax.axis_index("fsdp"), lax.axis_index("tensor")
    a = j + 1 - 2 * lax.rem(j, 2)
    b = lax.rem(j + 2, 4)
    opposite = 3 - j
    to_a, to_b, to_o = {"fsdp": a}, {"fsdp": b}, {"fsdp": opposite}
    to_sib = {"tensor": 1 - c}
    shard = basis_ref.shape[0]
    piece = shard // 8
    half = piece // 2
    tokens = act.shape[0]
    width = act.shape[1]
    owned = first_ref.shape[0]
    columns = weights_ref.shape[1]

    peers = [lax.rem(z + step, nz) for step in range(1, nz)]

    barrier = pltpu.get_barrier_semaphore()
    for target in [{"dp": peer} for peer in peers] + [to_a, to_b, to_o, to_sib]:
        pl.semaphore_signal(barrier, inc=1, device_id=target, device_id_type=MESH)
    pl.semaphore_wait(barrier, nz - 1 + 4)

    pending = []

    def push(src, dst, arrival, target):
        copy = pltpu.make_async_remote_copy(
            src_ref=src, dst_ref=dst, send_sem=send.at[len(pending)], recv_sem=arrival,
            device_id=target, device_id_type=MESH,
        )
        copy.start()
        pending.append(copy)

    def arrived(dst, arrival):
        pltpu.make_async_remote_copy(
            src_ref=dst, dst_ref=dst, send_sem=send.at[0], recv_sem=arrival,
            device_id=to_sib, device_id_type=MESH,
        ).wait_recv()

    def rows(zs, place, core, part=None):
        start = zs * shard + (place * 2 + core) * piece
        if part is None:
            return basis.at[pl.ds(pl.multiple_of(start, piece), piece)]
        return basis.at[pl.ds(pl.multiple_of(start + part * half, half), half)]

    def sem(kind, zs):
        return arrive_basis.at[kind * nz + zs]

    mine = basis_ref.at[pl.ds(pl.multiple_of((j * 2 + c) * piece, piece), piece)]
    for peer in peers:
        push(mine, rows(z, j, c), sem(FROM_Z, z), {"dp": peer})
    get_basis = pltpu.make_async_copy(
        basis_ref, basis.at[pl.ds(pl.multiple_of(z * shard, shard), shard)], local.at[0])
    get_act = pltpu.make_async_copy(
        act_ref.at[pl.ds(pl.multiple_of(c * tokens, tokens), tokens)], act, local.at[1])
    get_weights = pltpu.make_async_copy(weights_ref, weights_out.at[j], local.at[2])
    get_grads = pltpu.make_async_copy(grads_ref.at[j], grads.at[j], local.at[3])
    for copy in (get_basis, get_act, get_grads, get_weights):
        copy.start()
    for n, (place, target) in enumerate(((a, to_a), (b, to_b), (opposite, to_o))):
        push(grads_ref.at[place], grads.at[j], arrive_grads.at[n], target)

    def w_half(ref, part):
        return ref.at[:, pl.ds(part * (columns // 2), columns // 2)]

    def send_weights(part):
        push(w_half(weights_ref, part), w_half(weights_out.at[j], part), arrive_w.at[2 * part], to_a)
        push(w_half(weights_ref, part), w_half(weights_out.at[j], part), arrive_w.at[2 * part + 1], to_b)

    send_weights(0)

    def source(k):
        near = jnp.where(z < nz // 2, z, nz - 1 - z)
        s = jnp.where(k < near, k, k + 1)
        return jnp.where(z < nz // 2, s, nz - 1 - s)

    def forward(zs):
        arrived(rows(zs, a, c), sem(FROM_A, zs))
        push(rows(zs, a, c, 0), rows(zs, a, c, 0), sem(HALF0_B, zs), to_b)
        push(rows(zs, a, c), rows(zs, a, c), sem(SIB_A, zs), to_sib)
        arrived(rows(zs, b, c), sem(FROM_B, zs))
        push(rows(zs, b, c, 1), rows(zs, b, c, 1), sem(HALF1_A, zs), to_a)
        push(rows(zs, b, c), rows(zs, b, c), sem(SIB_B, zs), to_sib)

    def finish(zs):
        arrived(rows(zs, opposite, c, 0), sem(HALF0_B, zs))
        push(rows(zs, opposite, c, 0), rows(zs, opposite, c, 0), sem(SIB_H0, zs), to_sib)
        arrived(rows(zs, opposite, c, 1), sem(HALF1_A, zs))
        push(rows(zs, opposite, c, 1), rows(zs, opposite, c, 1), sem(SIB_H1, zs), to_sib)

    for k in range(nz - 1):
        zs = source(k)
        arrived(rows(zs, j, c), sem(FROM_Z, zs))
        push(rows(zs, j, c), rows(zs, j, c), sem(FROM_A, zs), to_a)
        push(rows(zs, j, c), rows(zs, j, c), sem(FROM_B, zs), to_b)
        push(rows(zs, j, c), rows(zs, j, c), sem(SIB_OWN, zs), to_sib)
        if k >= 1:
            forward(source(k - 1))
        if k >= 2:
            finish(source(k - 2))
    forward(source(nz - 2))
    if nz >= 3:
        finish(source(nz - 3))
    finish(source(nz - 2))

    arrived(w_half(weights_out.at[a], 0), arrive_w.at[0])
    push(w_half(weights_out.at[a], 0), w_half(weights_out.at[a], 0), arrive_w.at[4], to_b)

    for k in range(nz - 1):
        zs = source(k)
        arrived(rows(zs, j, 1 - c), sem(SIB_OWN, zs))
        arrived(rows(zs, a, 1 - c), sem(SIB_A, zs))
        arrived(rows(zs, b, 1 - c), sem(SIB_B, zs))
        arrived(rows(zs, opposite, 1 - c, 0), sem(SIB_H0, zs))
        arrived(rows(zs, opposite, 1 - c, 1), sem(SIB_H1, zs))
    get_basis.wait()
    get_act.wait()

    acc[...] = jnp.zeros_like(acc)
    depth = 512

    @pl.loop(0, width // depth)
    def _(k):
        at = pl.ds(pl.multiple_of(k * depth, depth), depth)
        acc[...] += jnp.dot(act[:, at], basis[at, :], preferred_element_type=F32)

    def low_rows(place, core):
        return low.at[place, pl.ds(pl.multiple_of(core * tokens, tokens), tokens)]

    low[j, pl.ds(pl.multiple_of(c * tokens, tokens), tokens), :] = acc[...].astype(BF16)
    for n, target in enumerate((to_a, to_b, to_o, to_sib)):
        push(low_rows(j, c), low_rows(j, c), arrive_low.at[n], target)
    put_basis = pltpu.make_async_copy(basis, basis_out, local.at[4])
    put_basis.start()
    send_weights(1)
    for n, place in enumerate((a, b, opposite)):
        arrived(low_rows(place, c), arrive_low.at[n])
        push(low_rows(place, c), low_rows(place, c), arrive_low.at[4 + n], to_sib)
    for n, place in ((3, j), (4, a), (5, b), (6, opposite)):
        arrived(low_rows(place, 1 - c), arrive_low.at[n])
    for n, place in enumerate((a, b, opposite)):
        arrived(grads.at[place], arrive_grads.at[n])
    get_grads.wait()

    def partial(peer):
        at = pl.ds(pl.multiple_of(peer * owned, owned), owned)
        total = jnp.dot(grads[0, at, :], low[0], preferred_element_type=F32)
        for place in range(1, 4):
            total += jnp.dot(grads[place, at, :], low[place], preferred_element_type=F32)
        return total

    @pl.loop(1, nz)
    def _(step):
        peer = lax.rem(z + step, nz)
        part_out[peer] = partial(peer).astype(BF16)

    for peer in peers:
        push(part_out.at[peer], part_in.at[z], arrive_part.at[z], {"dp": peer})
    part_own[...] = partial(z)

    for peer in peers:
        arrived(part_in.at[peer], arrive_part.at[peer])
        part_own[...] += part_in[peer].astype(F32)

    projected = part_own[...]
    first_new = beta_one * first_ref[...] + (1.0 - beta_one) * projected
    second_new = beta_two * second_ref[...] + (1.0 - beta_two) * projected * projected
    first_out[...] = first_new
    second_out[...] = second_new
    corrected = first_new / (1.0 - beta_one**STEP)
    scaled = jnp.sqrt(second_new / (1.0 - beta_two**STEP)) + epsilon
    direction[j] = (corrected / scaled).astype(BF16)
    for n, target in enumerate((to_a, to_b, to_o)):
        push(direction.at[j], direction.at[j], arrive_dir.at[n], target)

    arrived(w_half(weights_out.at[b], 1), arrive_w.at[3])
    push(w_half(weights_out.at[b], 1), w_half(weights_out.at[b], 1), arrive_w.at[5], to_a)
    for n, place in enumerate((a, b, opposite)):
        arrived(direction.at[place], arrive_dir.at[n])
    put_direction = pltpu.make_async_copy(direction, direction_out, local.at[5])
    put_direction.start()
    arrived(w_half(weights_out.at[b], 0), arrive_w.at[1])
    arrived(w_half(weights_out.at[a], 1), arrive_w.at[2])
    arrived(w_half(weights_out.at[opposite], 0), arrive_w.at[4])
    arrived(w_half(weights_out.at[opposite], 1), arrive_w.at[5])
    get_weights.wait()
    put_basis.wait()
    put_direction.wait()
    for copy in pending:
        copy.wait_send()


def shards(nz, activations, out_grads, basis, weights, first_moment, second_moment):
    tokens, width = activations.shape
    shard, rank = basis.shape
    owned = first_moment.shape[1]
    features = 4 * owned
    grads = out_grads[:, 0, :].reshape(tokens, nz, 4, owned)
    grads = grads.transpose(2, 1, 3, 0).reshape(4, nz * owned, tokens)
    vmem = pl.BlockSpec(memory_space=pltpu.VMEM)
    hbm = pl.BlockSpec(memory_space=pl.ANY)
    dma = pltpu.SemaphoreType.DMA
    sends = (nz - 1) * 11 + (nz - 1) + 3 + 6 + 7 + 3
    gathered, weight_rows, direction, first_new, second_new = pl.pallas_call(
        functools.partial(kernel, nz),
        out_shape=(
            jax.ShapeDtypeStruct((nz * shard, rank), BF16),
            jax.ShapeDtypeStruct((4, owned, width), BF16),
            jax.ShapeDtypeStruct((4, owned, rank), BF16),
            jax.ShapeDtypeStruct((owned, rank), F32),
            jax.ShapeDtypeStruct((owned, rank), F32),
        ),
        in_specs=[hbm, hbm, hbm, hbm, vmem, vmem],
        out_specs=(hbm, hbm, hbm, vmem, vmem),
        scratch_shapes=[
            pltpu.VMEM((tokens // 2, width), BF16),
            pltpu.VMEM((nz * shard, rank), BF16),
            pltpu.VMEM((4, nz * owned, tokens), BF16),
            pltpu.VMEM((4, tokens, rank), BF16),
            pltpu.VMEM((nz, owned, rank), BF16),
            pltpu.VMEM((nz, owned, rank), BF16),
            pltpu.VMEM((owned, rank), F32),
            pltpu.VMEM((4, owned, rank), BF16),
            pltpu.VMEM((tokens // 2, rank), F32),
            dma((6,)),
            dma((sends,)),
            dma((10 * nz,)),
            dma((3,)),
            dma((7,)),
            dma((nz,)),
            dma((3,)),
            dma((6,)),
        ],
        compiler_params=pltpu.CompilerParams(
            collective_id=0, has_side_effects=True, vmem_limit_bytes=50 * 2**20
        ),
        name="gather_and_step",
    )(activations, grads, basis, weights[0], first_moment[0], second_moment[0])
    update = lax.dot_general(
        direction.reshape(features, rank), gathered, (((1,), (1,)), ((), ())),
        preferred_element_type=F32,
    )
    rows = weight_rows.reshape(features, width)
    new_weights = (rows.astype(F32) - step_scale * update).astype(BF16)
    return (new_weights[None], first_new[None], second_new[None])


def solution(mesh):
    return jax.shard_map(
        functools.partial(shards, mesh.shape["dp"]),
        mesh=mesh,
        in_specs=(
            P(("dp", "fsdp"), None),
            P(("dp", "fsdp"), "tensor", None),
            P("dp", None),
            P("tensor", ("dp", "fsdp"), None),
            P("tensor", ("dp", "fsdp"), None),
            P("tensor", ("dp", "fsdp"), None),
        ),
        out_specs=(
            P("tensor", "dp", None),
            P("tensor", ("dp", "fsdp"), None),
            P("tensor", ("dp", "fsdp"), None),
        ),
        check_vma=False,
    )
```

```python
import functools

import jax
import jax.numpy as jnp
from jax import lax
from jax.experimental import pallas as pl
from jax.experimental.pallas import tpu as pltpu
from jax.sharding import PartitionSpec as P

STEP = 10
MESH = pl.DeviceIdType.MESH
F32 = jnp.float32
BF16 = jnp.bfloat16

beta_one = 0.9
beta_two = 0.999
epsilon = 1e-08
step_scale = 0.25

FROM_Z, FROM_A, FROM_B, HALF0_B, HALF1_A, SIB_OWN, SIB_A, SIB_B, SIB_H0, SIB_H1 = range(10)


def kernel(
    nz, act_ref, grads_ref, basis_ref, weights_ref, first_ref, second_ref,
    basis_out, weights_out, direction_out, first_out, second_out,
    act, basis, raw, turned, grads, low, part_out, part_in, part_own, direction, acc, first, second,
    local, hop, send, arrive_basis, arrive_grads, arrive_low, arrive_part, arrive_dir, arrive_w,
):
    z, j, c = lax.axis_index("dp"), lax.axis_index("fsdp"), lax.axis_index("tensor")
    a = j + 1 - 2 * lax.rem(j, 2)
    b = lax.rem(j + 2, 4)
    opposite = 3 - j
    to_a, to_b, to_o = {"fsdp": a}, {"fsdp": b}, {"fsdp": opposite}
    to_sib = {"tensor": 1 - c}
    shard = basis_ref.shape[0]
    piece = shard // 8
    half = piece // 2
    tokens = act.shape[0]
    width = act.shape[1]
    owned = first_ref.shape[0]
    columns = weights_ref.shape[1]

    peers = [lax.rem(z + step, nz) for step in range(1, nz)]

    barrier = pltpu.get_barrier_semaphore()
    for target in [{"dp": peer} for peer in peers] + [to_a, to_b, to_o, to_sib]:
        pl.semaphore_signal(barrier, inc=1, device_id=target, device_id_type=MESH)
    pl.semaphore_wait(barrier, nz - 1 + 4)

    pending = []

    def push(src, dst, arrival, target):
        copy = pltpu.make_async_remote_copy(
            src_ref=src, dst_ref=dst, send_sem=send.at[len(pending)], recv_sem=arrival,
            device_id=target, device_id_type=MESH,
        )
        copy.start()
        pending.append(copy)

    def arrived(dst, arrival):
        pltpu.make_async_remote_copy(
            src_ref=dst, dst_ref=dst, send_sem=send.at[0], recv_sem=arrival,
            device_id=to_sib, device_id_type=MESH,
        ).wait_recv()

    hops = []

    def relay(n, src, zs, target):
        inside = jnp.logical_and(target >= 0, target < nz)
        copy = pltpu.make_async_remote_copy(
            src_ref=src, dst_ref=rows(zs, j, c), send_sem=hop.at[n], recv_sem=sem(FROM_Z, zs),
            device_id={"dp": lax.rem(target + nz, nz)}, device_id_type=MESH,
        )
        pl.when(inside)(copy.start)
        hops.append((inside, copy))

    def rows(zs, place, core, part=None):
        start = zs * shard + (place * 2 + core) * piece
        if part is None:
            return basis.at[pl.ds(pl.multiple_of(start, piece), piece)]
        return basis.at[pl.ds(pl.multiple_of(start + part * half, half), half)]

    def sem(kind, zs):
        return arrive_basis.at[kind * nz + zs]

    mine = basis_ref.at[pl.ds(pl.multiple_of((j * 2 + c) * piece, piece), piece)]
    relay(0, mine, z, z + 1)
    relay(1, mine, z, z - 1)
    get_basis = pltpu.make_async_copy(
        basis_ref, basis.at[pl.ds(pl.multiple_of(z * shard, shard), shard)], local.at[0])
    get_act = pltpu.make_async_copy(
        act_ref.at[pl.ds(pl.multiple_of(c * tokens, tokens), tokens)], act, local.at[1])
    get_weights = pltpu.make_async_copy(weights_ref, weights_out.at[j], local.at[2])
    get_raw = pltpu.make_async_copy(grads_ref, raw, local.at[3])
    get_first = pltpu.make_async_copy(first_ref, first, local.at[6])
    get_second = pltpu.make_async_copy(second_ref, second, local.at[7])
    for copy in (get_raw, get_basis, get_act, get_weights, get_first, get_second):
        copy.start()

    get_raw.wait()
    for place in range(4):
        for zs in range(nz):
            begin = (zs * 4 + place) * owned
            turned[place, zs * owned : (zs + 1) * owned, :] = raw[:, begin : begin + owned].T
    for n, (place, target) in enumerate(((a, to_a), (b, to_b), (opposite, to_o))):
        push(turned.at[place], grads.at[j], arrive_grads.at[n], target)
    grads[j] = turned[j]

    def chunk(ref, n):
        return ref.at[:, pl.ds(n * (columns // 4), columns // 4)]

    def send_weights(n):
        push(chunk(weights_ref, n), chunk(weights_out.at[j], n), arrive_w.at[3 * n], to_a)
        push(chunk(weights_ref, n), chunk(weights_out.at[j], n), arrive_w.at[3 * n + 1], to_b)

    def forward_weights(n):
        came, way, target = (a, 0, to_b) if n % 2 == 0 else (b, 1, to_a)
        block = chunk(weights_out.at[came], n)
        arrived(block, arrive_w.at[3 * n + way])
        push(block, block, arrive_w.at[3 * n + 2], target)

    def finish_weights(n):
        came, way = (b, 1) if n % 2 == 0 else (a, 0)
        arrived(chunk(weights_out.at[came], n), arrive_w.at[3 * n + way])
        arrived(chunk(weights_out.at[opposite], n), arrive_w.at[3 * n + 2])

    def source(k):
        near = jnp.where(z < nz // 2, z, nz - 1 - z)
        s = jnp.where(k < near, k, k + 1)
        return jnp.where(z < nz // 2, s, nz - 1 - s)

    def forward(zs):
        arrived(rows(zs, a, c), sem(FROM_A, zs))
        push(rows(zs, a, c, 0), rows(zs, a, c, 0), sem(HALF0_B, zs), to_b)
        push(rows(zs, a, c), rows(zs, a, c), sem(SIB_A, zs), to_sib)
        arrived(rows(zs, b, c), sem(FROM_B, zs))
        push(rows(zs, b, c, 1), rows(zs, b, c, 1), sem(HALF1_A, zs), to_a)
        push(rows(zs, b, c), rows(zs, b, c), sem(SIB_B, zs), to_sib)

    def finish(zs):
        arrived(rows(zs, opposite, c, 0), sem(HALF0_B, zs))
        push(rows(zs, opposite, c, 0), rows(zs, opposite, c, 0), sem(SIB_H0, zs), to_sib)
        arrived(rows(zs, opposite, c, 1), sem(HALF1_A, zs))
        push(rows(zs, opposite, c, 1), rows(zs, opposite, c, 1), sem(SIB_H1, zs), to_sib)

    def collect(zs):
        arrived(rows(zs, j, 1 - c), sem(SIB_OWN, zs))
        arrived(rows(zs, a, 1 - c), sem(SIB_A, zs))
        arrived(rows(zs, b, 1 - c), sem(SIB_B, zs))
        arrived(rows(zs, opposite, 1 - c, 0), sem(SIB_H0, zs))
        arrived(rows(zs, opposite, 1 - c, 1), sem(SIB_H1, zs))

    depth = min(512, shard)

    def accumulate(zs):
        @pl.loop(0, shard // depth)
        def _(k):
            at = pl.ds(pl.multiple_of(zs * shard + k * depth, depth), depth)
            acc[...] += jnp.dot(act[:, at], basis[at, :], preferred_element_type=F32)

    for k in range(nz - 1):
        zs = source(k)
        arrived(rows(zs, j, c), sem(FROM_Z, zs))
        relay(2 + k, rows(zs, j, c), zs, jnp.where(zs < z, z + 1, z - 1))
        push(rows(zs, j, c), rows(zs, j, c), sem(FROM_A, zs), to_a)
        push(rows(zs, j, c), rows(zs, j, c), sem(FROM_B, zs), to_b)
        push(rows(zs, j, c), rows(zs, j, c), sem(SIB_OWN, zs), to_sib)
    for k in range(nz - 1):
        forward(source(k))
    send_weights(0)
    send_weights(1)
    get_basis.wait()
    get_act.wait()
    acc[...] = jnp.zeros_like(acc)
    accumulate(z)
    finish(source(0))
    for k in range(1, nz - 1):
        finish(source(k))
        collect(source(k - 1))
        accumulate(source(k - 1))
    collect(source(nz - 2))
    accumulate(source(nz - 2))

    def low_rows(place, core):
        return low.at[place, pl.ds(pl.multiple_of(core * tokens, tokens), tokens)]

    low[j, pl.ds(pl.multiple_of(c * tokens, tokens), tokens), :] = acc[...].astype(BF16)
    for n, target in enumerate((to_a, to_b, to_o, to_sib)):
        push(low_rows(j, c), low_rows(j, c), arrive_low.at[n], target)
    put_basis = pltpu.make_async_copy(basis, basis_out, local.at[4])
    put_basis.start()
    for n, place in enumerate((a, b, opposite)):
        arrived(low_rows(place, c), arrive_low.at[n])
        push(low_rows(place, c), low_rows(place, c), arrive_low.at[4 + n], to_sib)
    for n, place in ((3, j), (4, a), (5, b), (6, opposite)):
        arrived(low_rows(place, 1 - c), arrive_low.at[n])
    for n, place in enumerate((a, b, opposite)):
        arrived(grads.at[place], arrive_grads.at[n])
    forward_weights(0)
    forward_weights(1)
    send_weights(2)
    send_weights(3)

    def partial(peer):
        at = pl.ds(pl.multiple_of(peer * owned, owned), owned)
        total = jnp.dot(grads[0, at, :], low[0], preferred_element_type=F32)
        for place in range(1, 4):
            total += jnp.dot(grads[place, at, :], low[place], preferred_element_type=F32)
        return total

    @pl.loop(1, nz)
    def _(step):
        peer = lax.rem(z + step, nz)
        part_out[peer] = partial(peer).astype(BF16)

    for peer in peers:
        push(part_out.at[peer], part_in.at[z], arrive_part.at[z], {"dp": peer})
    part_own[...] = partial(z)

    for peer in peers:
        arrived(part_in.at[peer], arrive_part.at[peer])
        part_own[...] += part_in[peer].astype(F32)

    get_first.wait()
    get_second.wait()
    projected = part_own[...]
    first_new = beta_one * first[...] + (1.0 - beta_one) * projected
    second_new = beta_two * second[...] + (1.0 - beta_two) * projected * projected
    first_out[...] = first_new
    second_out[...] = second_new
    corrected = first_new / (1.0 - beta_one**STEP)
    scaled = jnp.sqrt(second_new / (1.0 - beta_two**STEP)) + epsilon
    direction[j] = (corrected / scaled).astype(BF16)
    for n, target in enumerate((to_a, to_b, to_o)):
        push(direction.at[j], direction.at[j], arrive_dir.at[n], target)

    forward_weights(2)
    forward_weights(3)
    for n, place in enumerate((a, b, opposite)):
        arrived(direction.at[place], arrive_dir.at[n])
    put_direction = pltpu.make_async_copy(direction, direction_out, local.at[5])
    put_direction.start()
    for n in range(4):
        finish_weights(n)
    get_weights.wait()
    put_basis.wait()
    put_direction.wait()
    for copy in pending:
        copy.wait_send()
    for inside, copy in hops:
        pl.when(inside)(copy.wait_send)


def renew(direction_ref, basis_ref, weights_ref, out_ref):
    update = lax.dot_general(
        direction_ref[...], basis_ref[...], (((1,), (1,)), ((), ())), preferred_element_type=F32
    )
    out_ref[...] = (weights_ref[...].astype(F32) - step_scale * update).astype(BF16)


def shards(nz, activations, out_grads, basis, weights, first_moment, second_moment):
    tokens, width = activations.shape
    shard, rank = basis.shape
    owned = first_moment.shape[1]
    features = 4 * owned
    vmem = pl.BlockSpec(memory_space=pltpu.VMEM)
    hbm = pl.BlockSpec(memory_space=pl.ANY)
    dma = pltpu.SemaphoreType.DMA
    sends = (nz - 1) * 9 + (nz - 1) + 3 + 12 + 7 + 3
    gathered, weight_rows, direction, first_new, second_new = pl.pallas_call(
        functools.partial(kernel, nz),
        out_shape=(
            jax.ShapeDtypeStruct((nz * shard, rank), BF16),
            jax.ShapeDtypeStruct((4, owned, width), BF16),
            jax.ShapeDtypeStruct((4, owned, rank), BF16),
            jax.ShapeDtypeStruct((owned, rank), F32),
            jax.ShapeDtypeStruct((owned, rank), F32),
        ),
        in_specs=[hbm] * 6,
        out_specs=(hbm, hbm, hbm, vmem, vmem),
        scratch_shapes=[
            pltpu.VMEM((tokens // 2, width), BF16),
            pltpu.VMEM((nz * shard, rank), BF16),
            pltpu.VMEM((tokens, 4 * nz * owned), BF16),
            pltpu.VMEM((4, nz * owned, tokens), BF16),
            pltpu.VMEM((4, nz * owned, tokens), BF16),
            pltpu.VMEM((4, tokens, rank), BF16),
            pltpu.VMEM((nz, owned, rank), BF16),
            pltpu.VMEM((nz, owned, rank), BF16),
            pltpu.VMEM((owned, rank), F32),
            pltpu.VMEM((4, owned, rank), BF16),
            pltpu.VMEM((tokens // 2, rank), F32),
            pltpu.VMEM((owned, rank), F32),
            pltpu.VMEM((owned, rank), F32),
            dma((8,)),
            dma((nz + 1,)),
            dma((sends,)),
            dma((10 * nz,)),
            dma((3,)),
            dma((7,)),
            dma((nz,)),
            dma((3,)),
            dma((12,)),
        ],
        compiler_params=pltpu.CompilerParams(
            collective_id=0, has_side_effects=True, vmem_limit_bytes=60 * 2**20
        ),
        name="gather_and_step",
    )(activations, out_grads[:, 0, :], basis, weights[0], first_moment[0], second_moment[0])
    block = 1024
    new_weights = pl.pallas_call(
        renew,
        out_shape=jax.ShapeDtypeStruct((features, width), BF16),
        grid=(width // block,),
        in_specs=[
            pl.BlockSpec((features, rank), lambda i: (0, 0)),
            pl.BlockSpec((block, rank), lambda i: (i, 0)),
            pl.BlockSpec((features, block), lambda i: (0, i)),
        ],
        out_specs=pl.BlockSpec((features, block), lambda i: (0, i)),
        compiler_params=pltpu.CompilerParams(vmem_limit_bytes=60 * 2**20),
        name="renew",
    )(direction.reshape(features, rank), gathered, weight_rows.reshape(features, width))
    return (new_weights[None], first_new[None], second_new[None])


def solution(mesh):
    return jax.shard_map(
        functools.partial(shards, mesh.shape["dp"]),
        mesh=mesh,
        in_specs=(
            P(("dp", "fsdp"), None),
            P(("dp", "fsdp"), "tensor", None),
            P("dp", None),
            P("tensor", ("dp", "fsdp"), None),
            P("tensor", ("dp", "fsdp"), None),
            P("tensor", ("dp", "fsdp"), None),
        ),
        out_specs=(
            P("tensor", "dp", None),
            P("tensor", ("dp", "fsdp"), None),
            P("tensor", ("dp", "fsdp"), None),
        ),
        check_vma=False,
    )
```

```python
import functools

import jax
import jax.numpy as jnp
from jax import lax
from jax.experimental import pallas as pl
from jax.experimental.pallas import tpu as pltpu
from jax.sharding import PartitionSpec as P

STEP = 10
MESH = pl.DeviceIdType.MESH
F32 = jnp.float32
BF16 = jnp.bfloat16

beta_one = 0.9
beta_two = 0.999
epsilon = 1e-08
step_scale = 0.25

FROM_Z, FROM_Z2, FROM_A, FROM_B, SIB_OWN, SIB_A, SIB_B, SIB_O = range(8)


def kernel(
    nz, act_ref, grads_ref, basis_ref, weights_ref, first_ref, second_ref,
    basis_out, weights_out, direction_out, first_out, second_out,
    act, basis, raw, turned, grads, low, part_out, part_in, part_own, direction, acc, first, second,
    local, hop, send, arrive_basis, arrive_grads, arrive_low, arrive_part, arrive_dir, arrive_w,
):
    z, j, c = lax.axis_index("dp"), lax.axis_index("fsdp"), lax.axis_index("tensor")
    a = j + 1 - 2 * lax.rem(j, 2)
    b = lax.rem(j + 2, 4)
    opposite = 3 - j
    to_a, to_b, to_o = {"fsdp": a}, {"fsdp": b}, {"fsdp": opposite}
    to_sib = {"tensor": 1 - c}
    shard = basis_ref.shape[0]
    piece = shard // 8
    tokens = act.shape[0]
    width = act.shape[1]
    owned = first_ref.shape[0]
    columns = weights_ref.shape[1]

    peers = [lax.rem(z + step, nz) for step in range(1, nz)]

    barrier = pltpu.get_barrier_semaphore()
    for target in [{"dp": peer} for peer in peers] + [to_a, to_b, to_o, to_sib]:
        pl.semaphore_signal(barrier, inc=1, device_id=target, device_id_type=MESH)
    pl.semaphore_wait(barrier, nz - 1 + 4)

    pending = []

    def push(src, dst, arrival, target):
        copy = pltpu.make_async_remote_copy(
            src_ref=src, dst_ref=dst, send_sem=send.at[len(pending)], recv_sem=arrival,
            device_id=target, device_id_type=MESH,
        )
        copy.start()
        pending.append(copy)

    def arrived(dst, arrival):
        pltpu.make_async_remote_copy(
            src_ref=dst, dst_ref=dst, send_sem=send.at[0], recv_sem=arrival,
            device_id=to_sib, device_id_type=MESH,
        ).wait_recv()

    hops = []

    def relay(src, zs, place, kind, target):
        inside = jnp.logical_and(target >= 0, target < nz)
        copy = pltpu.make_async_remote_copy(
            src_ref=src, dst_ref=rows(zs, place, c), send_sem=hop.at[len(hops)],
            recv_sem=sem(kind, zs), device_id={"dp": lax.rem(target + nz, nz)}, device_id_type=MESH,
        )
        pl.when(inside)(copy.start)
        hops.append((inside, copy))

    def rows(zs, place, core):
        start = zs * shard + (place * 2 + core) * piece
        return basis.at[pl.ds(pl.multiple_of(start, piece), piece)]

    def sem(kind, zs):
        return arrive_basis.at[kind * nz + zs]

    def start_own(place, kind):
        mine = basis_ref.at[pl.ds(pl.multiple_of((place * 2 + c) * piece, piece), piece)]
        relay(mine, z, place, kind, z + 1)
        relay(mine, z, place, kind, z - 1)

    start_own(j, FROM_Z)
    get_basis = pltpu.make_async_copy(
        basis_ref, basis.at[pl.ds(pl.multiple_of(z * shard, shard), shard)], local.at[0])
    get_act = pltpu.make_async_copy(
        act_ref.at[pl.ds(pl.multiple_of(c * tokens, tokens), tokens)], act, local.at[1])
    get_weights = pltpu.make_async_copy(weights_ref, weights_out.at[j], local.at[2])
    get_raw = pltpu.make_async_copy(grads_ref, raw, local.at[3])
    get_first = pltpu.make_async_copy(first_ref, first, local.at[6])
    get_second = pltpu.make_async_copy(second_ref, second, local.at[7])
    for copy in (get_raw, get_basis, get_act, get_weights, get_first, get_second):
        copy.start()

    get_raw.wait()
    for place in range(4):
        for zs in range(nz):
            begin = (zs * 4 + place) * owned
            turned[place, zs * owned : (zs + 1) * owned, :] = raw[:, begin : begin + owned].T
    for n, (place, target) in enumerate(((a, to_a), (b, to_b), (opposite, to_o))):
        push(turned.at[place], grads.at[j], arrive_grads.at[n], target)
    grads[j] = turned[j]

    def chunk(ref, n):
        return ref.at[:, pl.ds(n * (columns // 4), columns // 4)]

    def send_weights(n):
        push(chunk(weights_ref, n), chunk(weights_out.at[j], n), arrive_w.at[3 * n], to_a)
        push(chunk(weights_ref, n), chunk(weights_out.at[j], n), arrive_w.at[3 * n + 1], to_b)

    def forward_weights(n):
        came, way, target = (a, 0, to_b) if n % 2 == 0 else (b, 1, to_a)
        block = chunk(weights_out.at[came], n)
        arrived(block, arrive_w.at[3 * n + way])
        push(block, block, arrive_w.at[3 * n + 2], target)

    def finish_weights(n):
        came, way = (b, 1) if n % 2 == 0 else (a, 0)
        arrived(chunk(weights_out.at[came], n), arrive_w.at[3 * n + way])
        arrived(chunk(weights_out.at[opposite], n), arrive_w.at[3 * n + 2])

    def source(k):
        near = jnp.where(z < nz // 2, z, nz - 1 - z)
        s = jnp.where(k < near, k, k + 1)
        return jnp.where(z < nz // 2, s, nz - 1 - s)

    def to_sibling(zs, place, kind):
        push(rows(zs, place, c), rows(zs, place, c), sem(kind, zs), to_sib)

    def collect(zs):
        arrived(rows(zs, j, 1 - c), sem(SIB_OWN, zs))
        arrived(rows(zs, a, 1 - c), sem(SIB_A, zs))
        arrived(rows(zs, b, 1 - c), sem(SIB_B, zs))
        arrived(rows(zs, opposite, 1 - c), sem(SIB_O, zs))

    depth = min(512, shard)

    def accumulate(zs):
        @pl.loop(0, shard // depth)
        def _(k):
            at = pl.ds(pl.multiple_of(zs * shard + k * depth, depth), depth)
            acc[...] += jnp.dot(act[:, at], basis[at, :], preferred_element_type=F32)

    for k in range(nz - 1):
        zs = source(k)
        arrived(rows(zs, j, c), sem(FROM_Z, zs))
        relay(rows(zs, j, c), zs, j, FROM_Z, jnp.where(zs < z, z + 1, z - 1))
        push(rows(zs, j, c), rows(zs, j, c), sem(FROM_A, zs), to_a)
        push(rows(zs, j, c), rows(zs, j, c), sem(FROM_B, zs), to_b)
        to_sibling(zs, j, SIB_OWN)
    start_own(opposite, FROM_Z2)
    send_weights(0)
    send_weights(1)
    get_basis.wait()
    get_act.wait()
    acc[...] = jnp.zeros_like(acc)
    accumulate(z)
    for k in range(nz - 1):
        zs = source(k)
        if k == nz - 2:
            forward_weights(0)
            forward_weights(1)
            send_weights(2)
        arrived(rows(zs, a, c), sem(FROM_A, zs))
        to_sibling(zs, a, SIB_A)
        arrived(rows(zs, b, c), sem(FROM_B, zs))
        to_sibling(zs, b, SIB_B)
        arrived(rows(zs, opposite, c), sem(FROM_Z2, zs))
        relay(rows(zs, opposite, c), zs, opposite, FROM_Z2, jnp.where(zs < z, z + 1, z - 1))
        to_sibling(zs, opposite, SIB_O)
        if k >= 1:
            collect(source(k - 1))
            accumulate(source(k - 1))
    collect(source(nz - 2))
    accumulate(source(nz - 2))

    def low_rows(place, core):
        return low.at[place, pl.ds(pl.multiple_of(core * tokens, tokens), tokens)]

    low[j, pl.ds(pl.multiple_of(c * tokens, tokens), tokens), :] = acc[...].astype(BF16)
    for n, target in enumerate((to_a, to_b, to_o, to_sib)):
        push(low_rows(j, c), low_rows(j, c), arrive_low.at[n], target)
    put_basis = pltpu.make_async_copy(basis, basis_out, local.at[4])
    put_basis.start()
    for n, place in enumerate((a, b, opposite)):
        arrived(low_rows(place, c), arrive_low.at[n])
        push(low_rows(place, c), low_rows(place, c), arrive_low.at[4 + n], to_sib)
    for n, place in ((3, j), (4, a), (5, b), (6, opposite)):
        arrived(low_rows(place, 1 - c), arrive_low.at[n])
    for n, place in enumerate((a, b, opposite)):
        arrived(grads.at[place], arrive_grads.at[n])
    send_weights(3)
    forward_weights(2)

    def partial(peer):
        at = pl.ds(pl.multiple_of(peer * owned, owned), owned)
        total = jnp.dot(grads[0, at, :], low[0], preferred_element_type=F32)
        for place in range(1, 4):
            total += jnp.dot(grads[place, at, :], low[place], preferred_element_type=F32)
        return total

    @pl.loop(1, nz)
    def _(step):
        peer = lax.rem(z + step, nz)
        part_out[peer] = partial(peer).astype(BF16)

    for peer in peers:
        push(part_out.at[peer], part_in.at[z], arrive_part.at[z], {"dp": peer})
    part_own[...] = partial(z)
    forward_weights(3)

    for peer in peers:
        arrived(part_in.at[peer], arrive_part.at[peer])
        part_own[...] += part_in[peer].astype(F32)

    get_first.wait()
    get_second.wait()
    projected = part_own[...]
    first_new = beta_one * first[...] + (1.0 - beta_one) * projected
    second_new = beta_two * second[...] + (1.0 - beta_two) * projected * projected
    first_out[...] = first_new
    second_out[...] = second_new
    corrected = first_new / (1.0 - beta_one**STEP)
    scaled = jnp.sqrt(second_new / (1.0 - beta_two**STEP)) + epsilon
    direction[j] = (corrected / scaled).astype(BF16)
    for n, target in enumerate((to_a, to_b, to_o)):
        push(direction.at[j], direction.at[j], arrive_dir.at[n], target)

    for n, place in enumerate((a, b, opposite)):
        arrived(direction.at[place], arrive_dir.at[n])
    put_direction = pltpu.make_async_copy(direction, direction_out, local.at[5])
    put_direction.start()
    for n in range(4):
        finish_weights(n)
    get_weights.wait()
    put_basis.wait()
    put_direction.wait()
    for copy in pending:
        copy.wait_send()
    for inside, copy in hops:
        pl.when(inside)(copy.wait_send)


def renew(direction_ref, basis_ref, weights_ref, out_ref):
    step = 256
    for begin in range(0, out_ref.shape[1], step):
        at = slice(begin, begin + step)
        update = lax.dot_general(
            direction_ref[...], basis_ref[at, :], (((1,), (1,)), ((), ())),
            preferred_element_type=F32,
        )
        out_ref[:, at] = (weights_ref[:, at].astype(F32) - step_scale * update).astype(BF16)


def shards(nz, activations, out_grads, basis, weights, first_moment, second_moment):
    tokens, width = activations.shape
    shard, rank = basis.shape
    owned = first_moment.shape[1]
    features = 4 * owned
    vmem = pl.BlockSpec(memory_space=pltpu.VMEM)
    hbm = pl.BlockSpec(memory_space=pl.ANY)
    dma = pltpu.SemaphoreType.DMA
    sends = (nz - 1) * 6 + (nz - 1) + 3 + 12 + 7 + 3
    gathered, weight_rows, direction, first_new, second_new = pl.pallas_call(
        functools.partial(kernel, nz),
        out_shape=(
            jax.ShapeDtypeStruct((nz * shard, rank), BF16),
            jax.ShapeDtypeStruct((4, owned, width), BF16),
            jax.ShapeDtypeStruct((4, owned, rank), BF16),
            jax.ShapeDtypeStruct((owned, rank), F32),
            jax.ShapeDtypeStruct((owned, rank), F32),
        ),
        in_specs=[hbm] * 6,
        out_specs=(hbm, hbm, hbm, vmem, vmem),
        scratch_shapes=[
            pltpu.VMEM((tokens // 2, width), BF16),
            pltpu.VMEM((nz * shard, rank), BF16),
            pltpu.VMEM((tokens, 4 * nz * owned), BF16),
            pltpu.VMEM((4, nz * owned, tokens), BF16),
            pltpu.VMEM((4, nz * owned, tokens), BF16),
            pltpu.VMEM((4, tokens, rank), BF16),
            pltpu.VMEM((nz, owned, rank), BF16),
            pltpu.VMEM((nz, owned, rank), BF16),
            pltpu.VMEM((owned, rank), F32),
            pltpu.VMEM((4, owned, rank), BF16),
            pltpu.VMEM((tokens // 2, rank), F32),
            pltpu.VMEM((owned, rank), F32),
            pltpu.VMEM((owned, rank), F32),
            dma((8,)),
            dma((2 * (nz + 1),)),
            dma((sends,)),
            dma((8 * nz,)),
            dma((3,)),
            dma((7,)),
            dma((nz,)),
            dma((3,)),
            dma((12,)),
        ],
        compiler_params=pltpu.CompilerParams(
            collective_id=0, has_side_effects=True, vmem_limit_bytes=60 * 2**20
        ),
        name="gather_and_step",
    )(activations, out_grads[:, 0, :], basis, weights[0], first_moment[0], second_moment[0])
    block = 1024
    new_weights = pl.pallas_call(
        renew,
        out_shape=jax.ShapeDtypeStruct((features, width), BF16),
        grid=(width // block,),
        in_specs=[
            pl.BlockSpec((features, rank), lambda i: (0, 0)),
            pl.BlockSpec((block, rank), lambda i: (i, 0)),
            pl.BlockSpec((features, block), lambda i: (0, i)),
        ],
        out_specs=pl.BlockSpec((features, block), lambda i: (0, i)),
        compiler_params=pltpu.CompilerParams(vmem_limit_bytes=60 * 2**20),
        name="renew",
    )(direction.reshape(features, rank), gathered, weight_rows.reshape(features, width))
    return (new_weights[None], first_new[None], second_new[None])


def solution(mesh):
    return jax.shard_map(
        functools.partial(shards, mesh.shape["dp"]),
        mesh=mesh,
        in_specs=(
            P(("dp", "fsdp"), None),
            P(("dp", "fsdp"), "tensor", None),
            P("dp", None),
            P("tensor", ("dp", "fsdp"), None),
            P("tensor", ("dp", "fsdp"), None),
            P("tensor", ("dp", "fsdp"), None),
        ),
        out_specs=(
            P("tensor", "dp", None),
            P("tensor", ("dp", "fsdp"), None),
            P("tensor", ("dp", "fsdp"), None),
        ),
        check_vma=False,
    )
```

```python
import functools

import jax
import jax.numpy as jnp
from jax import lax
from jax.experimental import pallas as pl
from jax.experimental.pallas import tpu as pltpu
from jax.sharding import PartitionSpec as P

STEP = 10
MESH = pl.DeviceIdType.MESH
F32 = jnp.float32
BF16 = jnp.bfloat16

beta_one = 0.9
beta_two = 0.999
epsilon = 1e-08
step_scale = 0.25

FROM_Z, FROM_Z2, FROM_A, FROM_B, SIB_OWN, SIB_A, SIB_B, SIB_O = range(8)


def kernel(
    nz, act_ref, grads_ref, basis_ref, weights_ref, first_ref, second_ref,
    basis_out, weights_out, direction, first_out, second_out,
    act, basis, raw, turned, grads, low, part_out, part_in, part_own, acc, first, second,
    local, hop, send, arrive_basis, arrive_grads, arrive_low, arrive_part, arrive_dir, arrive_w,
):
    z, j, c = lax.axis_index("dp"), lax.axis_index("fsdp"), lax.axis_index("tensor")
    a = j + 1 - 2 * lax.rem(j, 2)
    b = lax.rem(j + 2, 4)
    opposite = 3 - j
    to_a, to_b, to_o = {"fsdp": a}, {"fsdp": b}, {"fsdp": opposite}
    to_sib = {"tensor": 1 - c}
    shard = basis_ref.shape[0]
    piece = shard // 8
    tokens = act.shape[0]
    width = act.shape[1]
    owned = first_ref.shape[0]
    columns = weights_ref.shape[1]

    peers = [lax.rem(z + step, nz) for step in range(1, nz)]

    barrier = pltpu.get_barrier_semaphore()
    for target in [{"dp": peer} for peer in peers] + [to_a, to_b, to_o, to_sib]:
        pl.semaphore_signal(barrier, inc=1, device_id=target, device_id_type=MESH)
    pl.semaphore_wait(barrier, nz - 1 + 4)

    pending = []

    def push(src, dst, arrival, target):
        copy = pltpu.make_async_remote_copy(
            src_ref=src, dst_ref=dst, send_sem=send.at[len(pending)], recv_sem=arrival,
            device_id=target, device_id_type=MESH,
        )
        copy.start()
        pending.append(copy)

    def arrived(dst, arrival):
        pltpu.make_async_remote_copy(
            src_ref=dst, dst_ref=dst, send_sem=send.at[0], recv_sem=arrival,
            device_id=to_sib, device_id_type=MESH,
        ).wait_recv()

    hops = []

    def relay(src, zs, place, kind, target):
        inside = jnp.logical_and(target >= 0, target < nz)
        copy = pltpu.make_async_remote_copy(
            src_ref=src, dst_ref=rows(zs, place, c), send_sem=hop.at[len(hops)],
            recv_sem=sem(kind, zs), device_id={"dp": lax.rem(target + nz, nz)}, device_id_type=MESH,
        )
        pl.when(inside)(copy.start)
        hops.append((inside, copy))

    def rows(zs, place, core):
        start = zs * shard + (place * 2 + core) * piece
        return basis.at[pl.ds(pl.multiple_of(start, piece), piece)]

    def sem(kind, zs):
        return arrive_basis.at[kind * nz + zs]

    def start_own(place, kind):
        mine = basis_ref.at[pl.ds(pl.multiple_of((place * 2 + c) * piece, piece), piece)]
        relay(mine, z, place, kind, z + 1)
        relay(mine, z, place, kind, z - 1)

    start_own(j, FROM_Z)
    get_basis = pltpu.make_async_copy(
        basis_ref, basis.at[pl.ds(pl.multiple_of(z * shard, shard), shard)], local.at[0])
    get_act = pltpu.make_async_copy(
        act_ref.at[pl.ds(pl.multiple_of(c * tokens, tokens), tokens)], act, local.at[1])
    get_weights = pltpu.make_async_copy(weights_ref, weights_out.at[j], local.at[2])
    get_raw = pltpu.make_async_copy(grads_ref, raw, local.at[3])
    get_first = pltpu.make_async_copy(first_ref, first, local.at[6])
    get_second = pltpu.make_async_copy(second_ref, second, local.at[7])
    for copy in (get_raw, get_basis, get_act, get_weights, get_first, get_second):
        copy.start()

    get_raw.wait()
    for place in range(4):
        for zs in range(nz):
            begin = (zs * 4 + place) * owned
            turned[place, zs * owned : (zs + 1) * owned, :] = raw[:, begin : begin + owned].T
    for n, (place, target) in enumerate(((a, to_a), (b, to_b), (opposite, to_o))):
        push(turned.at[place], grads.at[j], arrive_grads.at[n], target)
    grads[j] = turned[j]

    def chunk(ref, n):
        return ref.at[:, pl.ds(n * (columns // 4), columns // 4)]

    def send_weights(n):
        push(chunk(weights_ref, n), chunk(weights_out.at[j], n), arrive_w.at[3 * n], to_a)
        push(chunk(weights_ref, n), chunk(weights_out.at[j], n), arrive_w.at[3 * n + 1], to_b)

    def forward_weights(n):
        came, way, target = (a, 0, to_b) if n % 2 == 0 else (b, 1, to_a)
        block = chunk(weights_out.at[came], n)
        arrived(block, arrive_w.at[3 * n + way])
        push(block, block, arrive_w.at[3 * n + 2], target)

    def finish_weights(n):
        came, way = (b, 1) if n % 2 == 0 else (a, 0)
        arrived(chunk(weights_out.at[came], n), arrive_w.at[3 * n + way])
        arrived(chunk(weights_out.at[opposite], n), arrive_w.at[3 * n + 2])

    def source(k):
        near = jnp.where(z < nz // 2, z, nz - 1 - z)
        s = jnp.where(k < near, k, k + 1)
        return jnp.where(z < nz // 2, s, nz - 1 - s)

    def to_sibling(zs, place, kind):
        push(rows(zs, place, c), rows(zs, place, c), sem(kind, zs), to_sib)

    def collect(zs):
        arrived(rows(zs, j, 1 - c), sem(SIB_OWN, zs))
        arrived(rows(zs, a, 1 - c), sem(SIB_A, zs))
        arrived(rows(zs, b, 1 - c), sem(SIB_B, zs))
        arrived(rows(zs, opposite, 1 - c), sem(SIB_O, zs))

    depth = min(512, shard)

    def accumulate(zs):
        @pl.loop(0, shard // depth)
        def _(k):
            at = pl.ds(pl.multiple_of(zs * shard + k * depth, depth), depth)
            acc[...] += jnp.dot(act[:, at], basis[at, :], preferred_element_type=F32)

    for k in range(nz - 1):
        zs = source(k)
        arrived(rows(zs, j, c), sem(FROM_Z, zs))
        relay(rows(zs, j, c), zs, j, FROM_Z, jnp.where(zs < z, z + 1, z - 1))
        push(rows(zs, j, c), rows(zs, j, c), sem(FROM_A, zs), to_a)
        push(rows(zs, j, c), rows(zs, j, c), sem(FROM_B, zs), to_b)
        to_sibling(zs, j, SIB_OWN)
    start_own(opposite, FROM_Z2)
    send_weights(0)
    send_weights(1)
    get_basis.wait()
    get_act.wait()
    acc[...] = jnp.zeros_like(acc)
    accumulate(z)
    for k in range(nz - 1):
        zs = source(k)
        if k == nz - 2:
            forward_weights(0)
            forward_weights(1)
            send_weights(2)
        arrived(rows(zs, a, c), sem(FROM_A, zs))
        to_sibling(zs, a, SIB_A)
        arrived(rows(zs, b, c), sem(FROM_B, zs))
        to_sibling(zs, b, SIB_B)
        arrived(rows(zs, opposite, c), sem(FROM_Z2, zs))
        relay(rows(zs, opposite, c), zs, opposite, FROM_Z2, jnp.where(zs < z, z + 1, z - 1))
        to_sibling(zs, opposite, SIB_O)
        if k >= 1:
            collect(source(k - 1))
            accumulate(source(k - 1))
    collect(source(nz - 2))
    accumulate(source(nz - 2))

    parts = 2
    rank = basis.shape[1] // parts

    def cols(p):
        return pl.ds(p * rank, rank)

    def low_rows(place, core, p):
        return low.at[place, pl.ds(pl.multiple_of(core * tokens, tokens), tokens), cols(p)]

    low[j, pl.ds(pl.multiple_of(c * tokens, tokens), tokens), :] = acc[...].astype(BF16)
    for p in range(parts):
        for n, target in enumerate((to_a, to_b, to_o, to_sib)):
            push(low_rows(j, c, p), low_rows(j, c, p), arrive_low.at[7 * p + n], target)
    put_basis = pltpu.make_async_copy(basis, basis_out, local.at[4])
    put_basis.start()
    for n, place in enumerate((a, b, opposite)):
        arrived(grads.at[place], arrive_grads.at[n])

    def partial(peer, p):
        at = pl.ds(pl.multiple_of(peer * owned, owned), owned)
        total = jnp.dot(grads[0, at, :], low[0, :, cols(p)], preferred_element_type=F32)
        for place in range(1, 4):
            total += jnp.dot(grads[place, at, :], low[place, :, cols(p)], preferred_element_type=F32)
        return total

    def part_ref(ref, peer, p):
        return ref.at[peer, :, cols(p)]

    for p in range(parts):
        for n, place in enumerate((a, b, opposite)):
            arrived(low_rows(place, c, p), arrive_low.at[7 * p + n])
            push(low_rows(place, c, p), low_rows(place, c, p), arrive_low.at[7 * p + 4 + n], to_sib)
        if p == 0:
            send_weights(3)
            forward_weights(2)
        for n, place in ((3, j), (4, a), (5, b), (6, opposite)):
            arrived(low_rows(place, 1 - c, p), arrive_low.at[7 * p + n])

        @pl.loop(1, nz)
        def _(step):
            peer = lax.rem(z + step, nz)
            part_out[peer, :, cols(p)] = partial(peer, p).astype(BF16)

        for peer in peers:
            push(part_ref(part_out, peer, p), part_ref(part_in, z, p), arrive_part.at[p * nz + z], {"dp": peer})
        part_own[:, cols(p)] = partial(z, p)
    get_first.wait()
    get_second.wait()

    for p in range(parts):
        at = cols(p)
        for peer in peers:
            arrived(part_ref(part_in, peer, p), arrive_part.at[p * nz + peer])
            part_own[:, at] += part_in[peer, :, at].astype(F32)
        projected = part_own[:, at]
        first_new = beta_one * first[:, at] + (1.0 - beta_one) * projected
        second_new = beta_two * second[:, at] + (1.0 - beta_two) * projected * projected
        first_out[:, at] = first_new
        second_out[:, at] = second_new
        corrected = first_new / (1.0 - beta_one**STEP)
        scaled = jnp.sqrt(second_new / (1.0 - beta_two**STEP)) + epsilon
        direction[j, :, at] = (corrected / scaled).astype(BF16)
        for n, target in enumerate((to_a, to_b, to_o)):
            push(direction.at[j, :, at], direction.at[j, :, at], arrive_dir.at[3 * p + n], target)
        if p == 0:
            forward_weights(3)
    for p in range(parts):
        for n, place in enumerate((a, b, opposite)):
            arrived(direction.at[place, :, cols(p)], arrive_dir.at[3 * p + n])
    for n in range(4):
        finish_weights(n)
    get_weights.wait()
    put_basis.wait()
    for copy in pending:
        copy.wait_send()
    for inside, copy in hops:
        pl.when(inside)(copy.wait_send)


def renew(direction_ref, basis_ref, weights_ref, out_ref, tiles, ready, in_sems, out_sems):
    slots, block = tiles.shape[:2]
    steps = out_ref.shape[1] // block

    def at(t):
        return pl.ds(pl.multiple_of(t * block, block), block)

    def get(t, slot):
        return pltpu.make_async_copy(basis_ref.at[at(t)], tiles.at[slot], in_sems.at[slot])

    def put(t, slot):
        return pltpu.make_async_copy(ready.at[slot], out_ref.at[:, at(t)], out_sems.at[slot])

    for slot in range(slots):
        get(slot, slot).start()

    @pl.loop(0, steps // slots)
    def _(i):
        for slot in range(slots):
            t = slots * i + slot
            get(t, slot).wait()
            update = lax.dot_general(
                direction_ref[...], tiles[slot], (((1,), (1,)), ((), ())), preferred_element_type=F32
            )
            renewed = (weights_ref[:, at(t)].astype(F32) - step_scale * update).astype(BF16)
            pl.when(i > 0)(put(t, slot).wait)
            ready[slot] = renewed
            put(t, slot).start()
            pl.when(t + slots < steps)(get(t + slots, slot).start)

    for slot in range(slots):
        put(slot, slot).wait()


def shards(nz, activations, out_grads, basis, weights, first_moment, second_moment):
    tokens, width = activations.shape
    shard, rank = basis.shape
    owned = first_moment.shape[1]
    features = 4 * owned
    vmem = pl.BlockSpec(memory_space=pltpu.VMEM)
    hbm = pl.BlockSpec(memory_space=pltpu.HBM)
    dma = pltpu.SemaphoreType.DMA
    parts = 2
    sends = (nz - 1) * 6 + 3 + 12 + parts * (nz - 1 + 7 + 3)
    gathered, weight_rows, direction, first_new, second_new = pl.pallas_call(
        functools.partial(kernel, nz),
        out_shape=(
            jax.ShapeDtypeStruct((nz * shard, rank), BF16),
            pltpu.VMEM((4, owned, width), BF16),
            pltpu.VMEM((4, owned, rank), BF16),
            jax.ShapeDtypeStruct((owned, rank), F32),
            jax.ShapeDtypeStruct((owned, rank), F32),
        ),
        in_specs=[hbm] * 6,
        out_specs=(hbm, vmem, vmem, vmem, vmem),
        scratch_shapes=[
            pltpu.VMEM((tokens // 2, width), BF16),
            pltpu.VMEM((nz * shard, rank), BF16),
            pltpu.VMEM((tokens, 4 * nz * owned), BF16),
            pltpu.VMEM((4, nz * owned, tokens), BF16),
            pltpu.VMEM((4, nz * owned, tokens), BF16),
            pltpu.VMEM((4, tokens, rank), BF16),
            pltpu.VMEM((nz, owned, rank), BF16),
            pltpu.VMEM((nz, owned, rank), BF16),
            pltpu.VMEM((owned, rank), F32),
            pltpu.VMEM((tokens // 2, rank), F32),
            pltpu.VMEM((owned, rank), F32),
            pltpu.VMEM((owned, rank), F32),
            dma((8,)),
            dma((2 * (nz + 1),)),
            dma((sends,)),
            dma((8 * nz,)),
            dma((3,)),
            dma((parts * 7,)),
            dma((parts * nz,)),
            dma((parts * 3,)),
            dma((12,)),
        ],
        compiler_params=pltpu.CompilerParams(
            collective_id=0, has_side_effects=True, vmem_limit_bytes=46 * 2**20
        ),
        name="gather_and_step",
    )(activations, out_grads[:, 0, :], basis, weights[0], first_moment[0], second_moment[0])
    block = 512
    new_weights = pl.pallas_call(
        renew,
        out_shape=jax.ShapeDtypeStruct((features, width), BF16),
        in_specs=[vmem, hbm, vmem],
        out_specs=hbm,
        scratch_shapes=[
            pltpu.VMEM((4, block, rank), BF16),
            pltpu.VMEM((4, features, block), BF16),
            dma((4,)),
            dma((4,)),
        ],
        compiler_params=pltpu.CompilerParams(vmem_limit_bytes=46 * 2**20),
        name="renew",
    )(direction.reshape(features, rank), gathered, weight_rows.reshape(features, width))
    return (new_weights[None], first_new[None], second_new[None])


def solution(mesh):
    return jax.shard_map(
        functools.partial(shards, mesh.shape["dp"]),
        mesh=mesh,
        in_specs=(
            P(("dp", "fsdp"), None),
            P(("dp", "fsdp"), "tensor", None),
            P("dp", None),
            P("tensor", ("dp", "fsdp"), None),
            P("tensor", ("dp", "fsdp"), None),
            P("tensor", ("dp", "fsdp"), None),
        ),
        out_specs=(
            P("tensor", "dp", None),
            P("tensor", ("dp", "fsdp"), None),
            P("tensor", ("dp", "fsdp"), None),
        ),
        check_vma=False,
    )
```

```python
import functools

import jax
import jax.numpy as jnp
from jax import lax
from jax.experimental import pallas as pl
from jax.experimental.pallas import tpu as pltpu
from jax.sharding import PartitionSpec as P

STEP = 10
MESH = pl.DeviceIdType.MESH
F32 = jnp.float32
BF16 = jnp.bfloat16

beta_one = 0.9
beta_two = 0.999
epsilon = 1e-08
step_scale = 0.25

FROM_Z, FROM_Z2, FROM_A, FROM_B, SIB_OWN, SIB_A, SIB_B, SIB_O = range(8)


def kernel(
    nz, act_ref, grads_ref, basis_ref, weights_ref, first_ref, second_ref,
    basis_out, weights_out, direction_out, first_out, second_out,
    act, basis, raw, turned, grads, low, part_out, part_in, part_own, sums, direction, acc, first, second,
    local, hop, send, arrive_basis, arrive_grads, arrive_low, arrive_part, arrive_dir, arrive_w,
):
    z, j, c = lax.axis_index("dp"), lax.axis_index("fsdp"), lax.axis_index("tensor")
    a = j + 1 - 2 * lax.rem(j, 2)
    b = lax.rem(j + 2, 4)
    opposite = 3 - j
    to_a, to_b, to_o = {"fsdp": a}, {"fsdp": b}, {"fsdp": opposite}
    to_sib = {"tensor": 1 - c}
    shard = basis_ref.shape[0]
    piece = shard // 8
    tokens = act.shape[0]
    width = act.shape[1]
    owned = first_ref.shape[0]
    columns = weights_ref.shape[1]

    peers = [lax.rem(z + step, nz) for step in range(1, nz)]

    barrier = pltpu.get_barrier_semaphore()
    for target in [{"dp": peer} for peer in peers] + [to_a, to_b, to_o, to_sib]:
        pl.semaphore_signal(barrier, inc=1, device_id=target, device_id_type=MESH)
    pl.semaphore_wait(barrier, nz - 1 + 4)

    pending = []

    def push(src, dst, arrival, target):
        copy = pltpu.make_async_remote_copy(
            src_ref=src, dst_ref=dst, send_sem=send.at[len(pending)], recv_sem=arrival,
            device_id=target, device_id_type=MESH,
        )
        copy.start()
        pending.append(copy)

    def arrived(dst, arrival):
        pltpu.make_async_remote_copy(
            src_ref=dst, dst_ref=dst, send_sem=send.at[0], recv_sem=arrival,
            device_id=to_sib, device_id_type=MESH,
        ).wait_recv()

    hops = []

    def relay(src, zs, place, kind, target):
        inside = jnp.logical_and(target >= 0, target < nz)
        copy = pltpu.make_async_remote_copy(
            src_ref=src, dst_ref=rows(zs, place, c), send_sem=hop.at[len(hops)],
            recv_sem=sem(kind, zs), device_id={"dp": lax.rem(target + nz, nz)}, device_id_type=MESH,
        )
        pl.when(inside)(copy.start)
        hops.append((inside, copy))

    def rows(zs, place, core):
        start = zs * shard + (place * 2 + core) * piece
        return basis.at[pl.ds(pl.multiple_of(start, piece), piece)]

    def sem(kind, zs):
        return arrive_basis.at[kind * nz + zs]

    def start_own(place, kind):
        mine = basis_ref.at[pl.ds(pl.multiple_of((place * 2 + c) * piece, piece), piece)]
        relay(mine, z, place, kind, z + 1)
        relay(mine, z, place, kind, z - 1)

    start_own(j, FROM_Z)
    get_basis = pltpu.make_async_copy(
        basis_ref, basis.at[pl.ds(pl.multiple_of(z * shard, shard), shard)], local.at[0])
    get_act = pltpu.make_async_copy(
        act_ref.at[pl.ds(pl.multiple_of(c * tokens, tokens), tokens)], act, local.at[1])
    get_weights = pltpu.make_async_copy(weights_ref, weights_out.at[j], local.at[2])
    get_raw = pltpu.make_async_copy(grads_ref, raw, local.at[3])
    get_first = pltpu.make_async_copy(first_ref, first, local.at[6])
    get_second = pltpu.make_async_copy(second_ref, second, local.at[7])
    for copy in (get_raw, get_basis, get_act, get_weights, get_first, get_second):
        copy.start()

    get_raw.wait()
    for place in range(4):
        for zs in range(nz):
            begin = (zs * 4 + place) * owned
            turned[place, zs * owned : (zs + 1) * owned, :] = raw[:, begin : begin + owned].T
    for n, (place, target) in enumerate(((a, to_a), (b, to_b), (opposite, to_o))):
        push(turned.at[place], grads.at[j], arrive_grads.at[n], target)
    grads[j] = turned[j]

    def chunk(ref, n):
        return ref.at[:, pl.ds(n * (columns // 4), columns // 4)]

    def send_weights(n):
        push(chunk(weights_ref, n), chunk(weights_out.at[j], n), arrive_w.at[3 * n], to_a)
        push(chunk(weights_ref, n), chunk(weights_out.at[j], n), arrive_w.at[3 * n + 1], to_b)

    def forward_weights(n):
        came, way, target = (a, 0, to_b) if n % 2 == 0 else (b, 1, to_a)
        block = chunk(weights_out.at[came], n)
        arrived(block, arrive_w.at[3 * n + way])
        push(block, block, arrive_w.at[3 * n + 2], target)

    def finish_weights(n):
        came, way = (b, 1) if n % 2 == 0 else (a, 0)
        arrived(chunk(weights_out.at[came], n), arrive_w.at[3 * n + way])
        arrived(chunk(weights_out.at[opposite], n), arrive_w.at[3 * n + 2])

    def source(k):
        near = jnp.where(z < nz // 2, z, nz - 1 - z)
        s = jnp.where(k < near, k, k + 1)
        return jnp.where(z < nz // 2, s, nz - 1 - s)

    def to_sibling(zs, place, kind):
        push(rows(zs, place, c), rows(zs, place, c), sem(kind, zs), to_sib)

    def collect(zs):
        arrived(rows(zs, j, 1 - c), sem(SIB_OWN, zs))
        arrived(rows(zs, a, 1 - c), sem(SIB_A, zs))
        arrived(rows(zs, b, 1 - c), sem(SIB_B, zs))
        arrived(rows(zs, opposite, 1 - c), sem(SIB_O, zs))

    depth = min(512, shard)

    def accumulate(zs):
        @pl.loop(0, shard // depth)
        def _(k):
            at = pl.ds(pl.multiple_of(zs * shard + k * depth, depth), depth)
            acc[...] += jnp.dot(act[:, at], basis[at, :], preferred_element_type=F32)

    for k in range(nz - 1):
        zs = source(k)
        arrived(rows(zs, j, c), sem(FROM_Z, zs))
        relay(rows(zs, j, c), zs, j, FROM_Z, jnp.where(zs < z, z + 1, z - 1))
        push(rows(zs, j, c), rows(zs, j, c), sem(FROM_A, zs), to_a)
        push(rows(zs, j, c), rows(zs, j, c), sem(FROM_B, zs), to_b)
        to_sibling(zs, j, SIB_OWN)
    start_own(opposite, FROM_Z2)
    send_weights(0)
    send_weights(1)
    get_basis.wait()
    get_act.wait()
    acc[...] = jnp.zeros_like(acc)
    accumulate(z)
    for k in range(nz - 1):
        zs = source(k)
        if k == nz - 2:
            forward_weights(0)
            forward_weights(1)
            send_weights(2)
        arrived(rows(zs, opposite, c), sem(FROM_Z2, zs))
        relay(rows(zs, opposite, c), zs, opposite, FROM_Z2, jnp.where(zs < z, z + 1, z - 1))
        to_sibling(zs, opposite, SIB_O)
        arrived(rows(zs, a, c), sem(FROM_A, zs))
        to_sibling(zs, a, SIB_A)
        arrived(rows(zs, b, c), sem(FROM_B, zs))
        to_sibling(zs, b, SIB_B)
        if k >= 1:
            collect(source(k - 1))
            accumulate(source(k - 1))
    collect(source(nz - 2))
    accumulate(source(nz - 2))

    parts = 2
    rank = basis.shape[1] // parts

    def cols(p):
        return pl.ds(p * rank, rank)

    def low_rows(place, core, p):
        return low.at[place, pl.ds(pl.multiple_of(core * tokens, tokens), tokens), cols(p)]

    low[j, pl.ds(pl.multiple_of(c * tokens, tokens), tokens), :] = acc[...].astype(BF16)
    def low_half(place, core, p, side):
        at = pl.ds(p * rank + side * (rank // 2), rank // 2)
        return low.at[place, pl.ds(pl.multiple_of(core * tokens, tokens), tokens), at]

    for p in range(parts):
        for n, target in enumerate((to_a, to_b, to_sib)):
            push(low_rows(j, c, p), low_rows(j, c, p), arrive_low.at[9 * p + n], target)
    put_basis = pltpu.make_async_copy(basis, basis_out, local.at[4])
    put_basis.start()
    for n, place in enumerate((a, b, opposite)):
        arrived(grads.at[place], arrive_grads.at[n])

    def part_ref(ref, peer, p):
        return ref.at[peer, :, cols(p)]

    for p in range(parts):
        for n, place, target in ((0, a, to_b), (1, b, to_a)):
            arrived(low_rows(place, c, p), arrive_low.at[9 * p + n])
            onward = low_half(place, c, p, n)
            push(onward, onward, arrive_low.at[9 * p + 3 + n], target)
            push(low_rows(place, c, p), low_rows(place, c, p), arrive_low.at[9 * p + 5 + n], to_sib)
        if p == 0:
            send_weights(3)
            forward_weights(2)
        for side in range(2):
            corner = low_half(opposite, c, p, side)
            arrived(corner, arrive_low.at[9 * p + 3 + side])
            push(corner, corner, arrive_low.at[9 * p + 7 + side], to_sib)
        for n, place in ((2, j), (5, a), (6, b)):
            arrived(low_rows(place, 1 - c, p), arrive_low.at[9 * p + n])
        for side in range(2):
            arrived(low_half(opposite, 1 - c, p, side), arrive_low.at[9 * p + 7 + side])
        total = jnp.dot(grads[0], low[0, :, cols(p)], preferred_element_type=F32)
        for place in range(1, 4):
            total += jnp.dot(grads[place], low[place, :, cols(p)], preferred_element_type=F32)
        sums[...] = total
        for zs in range(nz):
            part_out[zs, :, cols(p)] = sums[zs * owned : (zs + 1) * owned, :].astype(BF16)

        for peer in peers:
            push(part_ref(part_out, peer, p), part_ref(part_in, z, p), arrive_part.at[p * nz + z], {"dp": peer})
        part_own[:, cols(p)] = sums[pl.ds(pl.multiple_of(z * owned, owned), owned), :]
    get_first.wait()
    get_second.wait()

    for p in range(parts):
        at = cols(p)
        for peer in peers:
            arrived(part_ref(part_in, peer, p), arrive_part.at[p * nz + peer])
            part_own[:, at] += part_in[peer, :, at].astype(F32)
        projected = part_own[:, at]
        first_new = beta_one * first[:, at] + (1.0 - beta_one) * projected
        second_new = beta_two * second[:, at] + (1.0 - beta_two) * projected * projected
        first_out[:, at] = first_new
        second_out[:, at] = second_new
        corrected = first_new / (1.0 - beta_one**STEP)
        scaled = jnp.sqrt(second_new / (1.0 - beta_two**STEP)) + epsilon
        direction[j, :, at] = (corrected / scaled).astype(BF16)
        for n, target in enumerate((to_a, to_b)):
            push(direction.at[j, :, at], direction.at[j, :, at], arrive_dir.at[4 * p + n], target)
        if p == 0:
            forward_weights(3)

    def direction_half(place, p, side):
        return direction.at[place, :, pl.ds(p * rank + side * (rank // 2), rank // 2)]

    for p in range(parts):
        for n, place, target in ((0, a, to_b), (1, b, to_a)):
            arrived(direction.at[place, :, cols(p)], arrive_dir.at[4 * p + n])
            onward = direction_half(place, p, n)
            push(onward, onward, arrive_dir.at[4 * p + 2 + n], target)
    for p in range(parts):
        for side in range(2):
            arrived(direction_half(opposite, p, side), arrive_dir.at[4 * p + 2 + side])
    put_direction = pltpu.make_async_copy(direction, direction_out, local.at[5])
    put_direction.start()
    for n in range(4):
        finish_weights(n)
    get_weights.wait()
    put_basis.wait()
    put_direction.wait()
    for copy in pending:
        copy.wait_send()
    for inside, copy in hops:
        pl.when(inside)(copy.wait_send)


def shards(nz, activations, out_grads, basis, weights, first_moment, second_moment):
    tokens, width = activations.shape
    shard, rank = basis.shape
    owned = first_moment.shape[1]
    features = 4 * owned
    vmem = pl.BlockSpec(memory_space=pltpu.VMEM)
    hbm = pl.BlockSpec(memory_space=pltpu.HBM)
    dma = pltpu.SemaphoreType.DMA
    parts = 2
    sends = (nz - 1) * 6 + 3 + 12 + parts * (nz - 1 + 9 + 4)
    gathered, weight_rows, direction, first_new, second_new = pl.pallas_call(
        functools.partial(kernel, nz),
        out_shape=(
            jax.ShapeDtypeStruct((nz * shard, rank), BF16),
            jax.ShapeDtypeStruct((4, owned, width), BF16),
            jax.ShapeDtypeStruct((4, owned, rank), BF16),
            jax.ShapeDtypeStruct((owned, rank), F32),
            jax.ShapeDtypeStruct((owned, rank), F32),
        ),
        in_specs=[hbm] * 6,
        out_specs=(hbm, hbm, hbm, vmem, vmem),
        scratch_shapes=[
            pltpu.VMEM((tokens // 2, width), BF16),
            pltpu.VMEM((nz * shard, rank), BF16),
            pltpu.VMEM((tokens, 4 * nz * owned), BF16),
            pltpu.VMEM((4, nz * owned, tokens), BF16),
            pltpu.VMEM((4, nz * owned, tokens), BF16),
            pltpu.VMEM((4, tokens, rank), BF16),
            pltpu.VMEM((nz, owned, rank), BF16),
            pltpu.VMEM((nz, owned, rank), BF16),
            pltpu.VMEM((owned, rank), F32),
            pltpu.VMEM((nz * owned, rank // parts), F32),
            pltpu.VMEM((4, owned, rank), BF16),
            pltpu.VMEM((tokens // 2, rank), F32),
            pltpu.VMEM((owned, rank), F32),
            pltpu.VMEM((owned, rank), F32),
            dma((8,)),
            dma((2 * (nz + 1),)),
            dma((sends,)),
            dma((8 * nz,)),
            dma((3,)),
            dma((parts * 9,)),
            dma((parts * nz,)),
            dma((parts * 4,)),
            dma((12,)),
        ],
        compiler_params=pltpu.CompilerParams(
            collective_id=0, has_side_effects=True, vmem_limit_bytes=60 * 2**20
        ),
        name="gather_and_step",
    )(activations, out_grads[:, 0, :], basis, weights[0], first_moment[0], second_moment[0])
    update = lax.dot_general(
        direction.reshape(features, rank), gathered, (((1,), (1,)), ((), ())),
        preferred_element_type=F32,
    )
    rows = weight_rows.reshape(features, width)
    new_weights = (rows.astype(F32) - step_scale * update).astype(BF16)
    return (new_weights[None], first_new[None], second_new[None])


def solution(mesh):
    return jax.shard_map(
        functools.partial(shards, mesh.shape["dp"]),
        mesh=mesh,
        in_specs=(
            P(("dp", "fsdp"), None),
            P(("dp", "fsdp"), "tensor", None),
            P("dp", None),
            P("tensor", ("dp", "fsdp"), None),
            P("tensor", ("dp", "fsdp"), None),
            P("tensor", ("dp", "fsdp"), None),
        ),
        out_specs=(
            P("tensor", "dp", None),
            P("tensor", ("dp", "fsdp"), None),
            P("tensor", ("dp", "fsdp"), None),
        ),
        check_vma=False,
    )
```

```python
import functools

import jax
import jax.numpy as jnp
from jax import lax
from jax.experimental import pallas as pl
from jax.experimental.pallas import tpu as pltpu
from jax.sharding import PartitionSpec as P

STEP = 10
MESH = pl.DeviceIdType.MESH
F32 = jnp.float32
BF16 = jnp.bfloat16

beta_one = 0.9
beta_two = 0.999
epsilon = 1e-08
step_scale = 0.25

FROM_Z, FROM_Z2, FROM_A, FROM_B, SIB_OWN, SIB_A, SIB_B, SIB_O = range(8)


def kernel(
    nz, act_ref, grads_ref, basis_ref, weights_ref, first_ref, second_ref,
    basis_out, weights_out, direction_out, first_out, second_out,
    act, basis, raw, turned, grads, low, part_out, part_in, part_own, sums, direction, acc, first, second,
    local, hop, send, arrive_basis, arrive_grads, arrive_low, arrive_part, arrive_dir, arrive_w,
):
    z, j, c = lax.axis_index("dp"), lax.axis_index("fsdp"), lax.axis_index("tensor")
    a = j + 1 - 2 * lax.rem(j, 2)
    b = lax.rem(j + 2, 4)
    opposite = 3 - j
    to_a, to_b, to_o = {"fsdp": a}, {"fsdp": b}, {"fsdp": opposite}
    to_sib = {"tensor": 1 - c}
    shard = basis_ref.shape[0]
    piece = shard // 8
    tokens = act.shape[0]
    width = act.shape[1]
    owned = first_ref.shape[0]
    columns = weights_ref.shape[1]

    peers = [lax.rem(z + step, nz) for step in range(1, nz)]

    barrier = pltpu.get_barrier_semaphore()
    for target in [{"dp": peer} for peer in peers] + [to_a, to_b, to_o, to_sib]:
        pl.semaphore_signal(barrier, inc=1, device_id=target, device_id_type=MESH)
    pl.semaphore_wait(barrier, nz - 1 + 4)

    pending = []

    def push(src, dst, arrival, target):
        copy = pltpu.make_async_remote_copy(
            src_ref=src, dst_ref=dst, send_sem=send.at[len(pending)], recv_sem=arrival,
            device_id=target, device_id_type=MESH,
        )
        copy.start()
        pending.append(copy)

    def arrived(dst, arrival):
        pltpu.make_async_remote_copy(
            src_ref=dst, dst_ref=dst, send_sem=send.at[0], recv_sem=arrival,
            device_id=to_sib, device_id_type=MESH,
        ).wait_recv()

    hops = []

    def relay(src, zs, place, kind, target):
        inside = jnp.logical_and(target >= 0, target < nz)
        copy = pltpu.make_async_remote_copy(
            src_ref=src, dst_ref=rows(zs, place, c), send_sem=hop.at[len(hops)],
            recv_sem=sem(kind, zs), device_id={"dp": lax.rem(target + nz, nz)}, device_id_type=MESH,
        )
        pl.when(inside)(copy.start)
        hops.append((inside, copy))

    def rows(zs, place, core):
        start = zs * shard + (place * 2 + core) * piece
        return basis.at[pl.ds(pl.multiple_of(start, piece), piece)]

    def sem(kind, zs):
        return arrive_basis.at[kind * nz + zs]

    def start_own(place, kind):
        mine = basis_ref.at[pl.ds(pl.multiple_of((place * 2 + c) * piece, piece), piece)]
        relay(mine, z, place, kind, z + 1)
        relay(mine, z, place, kind, z - 1)

    start_own(j, FROM_Z)
    get_basis = pltpu.make_async_copy(
        basis_ref, basis.at[pl.ds(pl.multiple_of(z * shard, shard), shard)], local.at[0])
    get_act = pltpu.make_async_copy(
        act_ref.at[pl.ds(pl.multiple_of(c * tokens, tokens), tokens)], act, local.at[1])
    get_weights = pltpu.make_async_copy(weights_ref, weights_out.at[j], local.at[2])
    get_raw = pltpu.make_async_copy(grads_ref, raw, local.at[3])
    get_first = pltpu.make_async_copy(first_ref, first, local.at[6])
    get_second = pltpu.make_async_copy(second_ref, second, local.at[7])
    for copy in (get_raw, get_basis, get_act, get_weights, get_first, get_second):
        copy.start()

    get_raw.wait()
    for place in range(4):
        for zs in range(nz):
            begin = (zs * 4 + place) * owned
            turned[place, zs * owned : (zs + 1) * owned, :] = raw[:, begin : begin + owned].T
    for n, (place, target) in enumerate(((a, to_a), (b, to_b), (opposite, to_o))):
        push(turned.at[place], grads.at[j], arrive_grads.at[n], target)
    grads[j] = turned[j]

    def chunk(ref, n):
        return ref.at[:, pl.ds(n * (columns // 4), columns // 4)]

    def send_weights(n):
        push(chunk(weights_ref, n), chunk(weights_out.at[j], n), arrive_w.at[3 * n], to_a)
        push(chunk(weights_ref, n), chunk(weights_out.at[j], n), arrive_w.at[3 * n + 1], to_b)

    def forward_weights(n):
        came, way, target = (a, 0, to_b) if n % 2 == 0 else (b, 1, to_a)
        block = chunk(weights_out.at[came], n)
        arrived(block, arrive_w.at[3 * n + way])
        push(block, block, arrive_w.at[3 * n + 2], target)

    def finish_weights(n):
        came, way = (b, 1) if n % 2 == 0 else (a, 0)
        arrived(chunk(weights_out.at[came], n), arrive_w.at[3 * n + way])
        arrived(chunk(weights_out.at[opposite], n), arrive_w.at[3 * n + 2])

    def source(k):
        near = jnp.where(z < nz // 2, z, nz - 1 - z)
        s = jnp.where(k < near, k, k + 1)
        return jnp.where(z < nz // 2, s, nz - 1 - s)

    def to_sibling(zs, place, kind):
        push(rows(zs, place, c), rows(zs, place, c), sem(kind, zs), to_sib)

    def collect(zs):
        arrived(rows(zs, j, 1 - c), sem(SIB_OWN, zs))
        arrived(rows(zs, a, 1 - c), sem(SIB_A, zs))
        arrived(rows(zs, b, 1 - c), sem(SIB_B, zs))
        arrived(rows(zs, opposite, 1 - c), sem(SIB_O, zs))

    depth = min(512, shard)

    def accumulate(zs):
        @pl.loop(0, shard // depth)
        def _(k):
            at = pl.ds(pl.multiple_of(zs * shard + k * depth, depth), depth)
            acc[...] += jnp.dot(act[:, at], basis[at, :], preferred_element_type=F32)

    for k in range(nz - 1):
        zs = source(k)
        arrived(rows(zs, j, c), sem(FROM_Z, zs))
        relay(rows(zs, j, c), zs, j, FROM_Z, jnp.where(zs < z, z + 1, z - 1))
        push(rows(zs, j, c), rows(zs, j, c), sem(FROM_A, zs), to_a)
        push(rows(zs, j, c), rows(zs, j, c), sem(FROM_B, zs), to_b)
        to_sibling(zs, j, SIB_OWN)
    start_own(opposite, FROM_Z2)
    send_weights(0)
    send_weights(1)
    get_basis.wait()
    get_act.wait()
    acc[...] = jnp.zeros_like(acc)
    accumulate(z)
    for k in range(nz - 1):
        zs = source(k)
        arrived(rows(zs, opposite, c), sem(FROM_Z2, zs))
        relay(rows(zs, opposite, c), zs, opposite, FROM_Z2, jnp.where(zs < z, z + 1, z - 1))
        to_sibling(zs, opposite, SIB_O)
        arrived(rows(zs, a, c), sem(FROM_A, zs))
        to_sibling(zs, a, SIB_A)
        arrived(rows(zs, b, c), sem(FROM_B, zs))
        to_sibling(zs, b, SIB_B)
        if k == nz - 2:
            forward_weights(0)
            forward_weights(1)
        if k >= 1:
            collect(source(k - 1))
            accumulate(source(k - 1))
    collect(source(nz - 2))
    accumulate(source(nz - 2))

    parts = 2
    rank = basis.shape[1] // parts

    def cols(p):
        return pl.ds(p * rank, rank)

    def low_rows(place, core, p):
        return low.at[place, pl.ds(pl.multiple_of(core * tokens, tokens), tokens), cols(p)]

    low[j, pl.ds(pl.multiple_of(c * tokens, tokens), tokens), :] = acc[...].astype(BF16)
    for p in range(parts):
        for n, target in enumerate((to_a, to_b, to_o, to_sib)):
            push(low_rows(j, c, p), low_rows(j, c, p), arrive_low.at[7 * p + n], target)
    put_basis = pltpu.make_async_copy(basis, basis_out, local.at[4])
    put_basis.start()
    for n, place in enumerate((a, b, opposite)):
        arrived(grads.at[place], arrive_grads.at[n])

    def part_ref(ref, peer, p):
        return ref.at[peer, :, cols(p)]

    for p in range(parts):
        for n, place in enumerate((a, b, opposite)):
            arrived(low_rows(place, c, p), arrive_low.at[7 * p + n])
            push(low_rows(place, c, p), low_rows(place, c, p), arrive_low.at[7 * p + 4 + n], to_sib)
        if p == 0:
            send_weights(2)
            send_weights(3)
        for n, place in ((3, j), (4, a), (5, b), (6, opposite)):
            arrived(low_rows(place, 1 - c, p), arrive_low.at[7 * p + n])
        total = jnp.dot(grads[0], low[0, :, cols(p)], preferred_element_type=F32)
        for place in range(1, 4):
            total += jnp.dot(grads[place], low[place, :, cols(p)], preferred_element_type=F32)
        sums[...] = total
        for zs in range(nz):
            part_out[zs, :, cols(p)] = sums[zs * owned : (zs + 1) * owned, :].astype(BF16)

        for peer in peers:
            push(part_ref(part_out, peer, p), part_ref(part_in, z, p), arrive_part.at[p * nz + z], {"dp": peer})
        part_own[:, cols(p)] = sums[pl.ds(pl.multiple_of(z * owned, owned), owned), :]
    forward_weights(2)
    get_first.wait()
    get_second.wait()

    for p in range(parts):
        at = cols(p)
        for peer in peers:
            arrived(part_ref(part_in, peer, p), arrive_part.at[p * nz + peer])
            part_own[:, at] += part_in[peer, :, at].astype(F32)
        projected = part_own[:, at]
        first_new = beta_one * first[:, at] + (1.0 - beta_one) * projected
        second_new = beta_two * second[:, at] + (1.0 - beta_two) * projected * projected
        first_out[:, at] = first_new
        second_out[:, at] = second_new
        corrected = first_new / (1.0 - beta_one**STEP)
        scaled = jnp.sqrt(second_new / (1.0 - beta_two**STEP)) + epsilon
        direction[j, :, at] = (corrected / scaled).astype(BF16)
        for n, target in enumerate((to_a, to_b, to_o)):
            push(direction.at[j, :, at], direction.at[j, :, at], arrive_dir.at[3 * p + n], target)
    forward_weights(3)
    for p in range(parts):
        for n, place in enumerate((a, b, opposite)):
            arrived(direction.at[place, :, cols(p)], arrive_dir.at[3 * p + n])
    put_direction = pltpu.make_async_copy(direction, direction_out, local.at[5])
    put_direction.start()
    for n in range(4):
        finish_weights(n)
    get_weights.wait()
    put_basis.wait()
    put_direction.wait()
    for copy in pending:
        copy.wait_send()
    for inside, copy in hops:
        pl.when(inside)(copy.wait_send)


def shards(nz, activations, out_grads, basis, weights, first_moment, second_moment):
    tokens, width = activations.shape
    shard, rank = basis.shape
    owned = first_moment.shape[1]
    features = 4 * owned
    vmem = pl.BlockSpec(memory_space=pltpu.VMEM)
    hbm = pl.BlockSpec(memory_space=pltpu.HBM)
    dma = pltpu.SemaphoreType.DMA
    parts = 2
    sends = (nz - 1) * 6 + 3 + 12 + parts * (nz - 1 + 7 + 3)
    gathered, weight_rows, direction, first_new, second_new = pl.pallas_call(
        functools.partial(kernel, nz),
        out_shape=(
            jax.ShapeDtypeStruct((nz * shard, rank), BF16),
            jax.ShapeDtypeStruct((4, owned, width), BF16),
            jax.ShapeDtypeStruct((4, owned, rank), BF16),
            jax.ShapeDtypeStruct((owned, rank), F32),
            jax.ShapeDtypeStruct((owned, rank), F32),
        ),
        in_specs=[hbm] * 6,
        out_specs=(hbm, hbm, hbm, vmem, vmem),
        scratch_shapes=[
            pltpu.VMEM((tokens // 2, width), BF16),
            pltpu.VMEM((nz * shard, rank), BF16),
            pltpu.VMEM((tokens, 4 * nz * owned), BF16),
            pltpu.VMEM((4, nz * owned, tokens), BF16),
            pltpu.VMEM((4, nz * owned, tokens), BF16),
            pltpu.VMEM((4, tokens, rank), BF16),
            pltpu.VMEM((nz, owned, rank), BF16),
            pltpu.VMEM((nz, owned, rank), BF16),
            pltpu.VMEM((owned, rank), F32),
            pltpu.VMEM((nz * owned, rank // parts), F32),
            pltpu.VMEM((4, owned, rank), BF16),
            pltpu.VMEM((tokens // 2, rank), F32),
            pltpu.VMEM((owned, rank), F32),
            pltpu.VMEM((owned, rank), F32),
            dma((8,)),
            dma((2 * (nz + 1),)),
            dma((sends,)),
            dma((8 * nz,)),
            dma((3,)),
            dma((parts * 7,)),
            dma((parts * nz,)),
            dma((parts * 3,)),
            dma((12,)),
        ],
        compiler_params=pltpu.CompilerParams(
            collective_id=0, has_side_effects=True, vmem_limit_bytes=60 * 2**20
        ),
        name="gather_and_step",
    )(activations, out_grads[:, 0, :], basis, weights[0], first_moment[0], second_moment[0])
    update = lax.dot_general(
        direction.reshape(features, rank), gathered, (((1,), (1,)), ((), ())),
        preferred_element_type=F32,
    )
    rows = weight_rows.reshape(features, width)
    new_weights = (rows.astype(F32) - step_scale * update).astype(BF16)
    return (new_weights[None], first_new[None], second_new[None])


def solution(mesh):
    return jax.shard_map(
        functools.partial(shards, mesh.shape["dp"]),
        mesh=mesh,
        in_specs=(
            P(("dp", "fsdp"), None),
            P(("dp", "fsdp"), "tensor", None),
            P("dp", None),
            P("tensor", ("dp", "fsdp"), None),
            P("tensor", ("dp", "fsdp"), None),
            P("tensor", ("dp", "fsdp"), None),
        ),
        out_specs=(
            P("tensor", "dp", None),
            P("tensor", ("dp", "fsdp"), None),
            P("tensor", ("dp", "fsdp"), None),
        ),
        check_vma=False,
    )
```

```python
import functools

import jax
import jax.numpy as jnp
from jax import lax
from jax.experimental import pallas as pl
from jax.experimental.pallas import tpu as pltpu
from jax.sharding import PartitionSpec as P

STEP = 10
MESH = pl.DeviceIdType.MESH
F32 = jnp.float32
BF16 = jnp.bfloat16

beta_one = 0.9
beta_two = 0.999
epsilon = 1e-08
step_scale = 0.25

FROM_Z, FROM_Z2, FROM_A, FROM_B, SIB_OWN, SIB_A, SIB_B, SIB_O = range(8)


def kernel(
    nz, act_ref, grads_ref, basis_ref, weights_ref, first_ref, second_ref,
    basis_out, weights_out, direction_out, first_out, second_out,
    act, basis, raw, turned, grads, low, part_out, part_in, part_own, sums, direction, acc, first, second,
    local, hop, send, arrive_basis, arrive_grads, arrive_low, arrive_part, arrive_dir, arrive_w,
):
    z, j, c = lax.axis_index("dp"), lax.axis_index("fsdp"), lax.axis_index("tensor")
    a = j + 1 - 2 * lax.rem(j, 2)
    b = lax.rem(j + 2, 4)
    opposite = 3 - j
    to_a, to_b, to_o = {"fsdp": a}, {"fsdp": b}, {"fsdp": opposite}
    to_sib = {"tensor": 1 - c}
    shard = basis_ref.shape[0]
    piece = shard // 8
    tokens = act.shape[0]
    width = act.shape[1]
    owned = first_ref.shape[0]
    columns = weights_ref.shape[1]

    peers = [lax.rem(z + step, nz) for step in range(1, nz)]

    barrier = pltpu.get_barrier_semaphore()
    for target in [{"dp": peer} for peer in peers] + [to_a, to_b, to_o, to_sib]:
        pl.semaphore_signal(barrier, inc=1, device_id=target, device_id_type=MESH)
    pl.semaphore_wait(barrier, nz - 1 + 4)

    pending = []

    def push(src, dst, arrival, target):
        copy = pltpu.make_async_remote_copy(
            src_ref=src, dst_ref=dst, send_sem=send.at[len(pending)], recv_sem=arrival,
            device_id=target, device_id_type=MESH,
        )
        copy.start()
        pending.append(copy)

    def arrived(dst, arrival):
        pltpu.make_async_remote_copy(
            src_ref=dst, dst_ref=dst, send_sem=send.at[0], recv_sem=arrival,
            device_id=to_sib, device_id_type=MESH,
        ).wait_recv()

    hops = []

    def relay(src, zs, place, kind, target):
        inside = jnp.logical_and(target >= 0, target < nz)
        copy = pltpu.make_async_remote_copy(
            src_ref=src, dst_ref=rows(zs, place, c), send_sem=hop.at[len(hops)],
            recv_sem=sem(kind, zs), device_id={"dp": lax.rem(target + nz, nz)}, device_id_type=MESH,
        )
        pl.when(inside)(copy.start)
        hops.append((inside, copy))

    def rows(zs, place, core):
        start = zs * shard + (place * 2 + core) * piece
        return basis.at[pl.ds(pl.multiple_of(start, piece), piece)]

    def sem(kind, zs):
        return arrive_basis.at[kind * nz + zs]

    def start_own(place, kind):
        mine = basis_ref.at[pl.ds(pl.multiple_of((place * 2 + c) * piece, piece), piece)]
        relay(mine, z, place, kind, z + 1)
        relay(mine, z, place, kind, z - 1)

    start_own(j, FROM_Z)
    get_basis = pltpu.make_async_copy(
        basis_ref, basis.at[pl.ds(pl.multiple_of(z * shard, shard), shard)], local.at[0])
    get_act = pltpu.make_async_copy(
        act_ref.at[pl.ds(pl.multiple_of(c * tokens, tokens), tokens)], act, local.at[1])
    get_weights = pltpu.make_async_copy(weights_ref, weights_out.at[j], local.at[2])
    get_raw = pltpu.make_async_copy(grads_ref, raw, local.at[3])
    get_first = pltpu.make_async_copy(first_ref, first, local.at[6])
    get_second = pltpu.make_async_copy(second_ref, second, local.at[7])
    for copy in (get_raw, get_basis, get_act, get_weights, get_first, get_second):
        copy.start()

    get_raw.wait()
    for place in range(4):
        for zs in range(nz):
            begin = (zs * 4 + place) * owned
            turned[place, zs * owned : (zs + 1) * owned, :] = raw[:, begin : begin + owned].T
    for n, (place, target) in enumerate(((a, to_a), (b, to_b), (opposite, to_o))):
        push(turned.at[place], grads.at[j], arrive_grads.at[n], target)
    grads[j] = turned[j]

    def chunk(ref, n):
        return ref.at[:, pl.ds(n * (columns // 4), columns // 4)]

    def send_weights(n):
        push(chunk(weights_ref, n), chunk(weights_out.at[j], n), arrive_w.at[3 * n], to_a)
        push(chunk(weights_ref, n), chunk(weights_out.at[j], n), arrive_w.at[3 * n + 1], to_b)

    def forward_weights(n):
        came, way, target = (a, 0, to_b) if n % 2 == 0 else (b, 1, to_a)
        block = chunk(weights_out.at[came], n)
        arrived(block, arrive_w.at[3 * n + way])
        push(block, block, arrive_w.at[3 * n + 2], target)

    def finish_weights(n):
        came, way = (b, 1) if n % 2 == 0 else (a, 0)
        arrived(chunk(weights_out.at[came], n), arrive_w.at[3 * n + way])
        arrived(chunk(weights_out.at[opposite], n), arrive_w.at[3 * n + 2])

    def source(k):
        near = jnp.where(z < nz // 2, z, nz - 1 - z)
        s = jnp.where(k < near, k, k + 1)
        return jnp.where(z < nz // 2, s, nz - 1 - s)

    def to_sibling(zs, place, kind):
        push(rows(zs, place, c), rows(zs, place, c), sem(kind, zs), to_sib)

    def collect(zs):
        arrived(rows(zs, j, 1 - c), sem(SIB_OWN, zs))
        arrived(rows(zs, a, 1 - c), sem(SIB_A, zs))
        arrived(rows(zs, b, 1 - c), sem(SIB_B, zs))
        arrived(rows(zs, opposite, 1 - c), sem(SIB_O, zs))

    depth = min(512, shard)

    def accumulate(zs):
        @pl.loop(0, shard // depth)
        def _(k):
            at = pl.ds(pl.multiple_of(zs * shard + k * depth, depth), depth)
            acc[...] += jnp.dot(act[:, at], basis[at, :], preferred_element_type=F32)

    for k in range(nz - 1):
        zs = source(k)
        arrived(rows(zs, j, c), sem(FROM_Z, zs))
        relay(rows(zs, j, c), zs, j, FROM_Z, jnp.where(zs < z, z + 1, z - 1))
        push(rows(zs, j, c), rows(zs, j, c), sem(FROM_A, zs), to_a)
        push(rows(zs, j, c), rows(zs, j, c), sem(FROM_B, zs), to_b)
        to_sibling(zs, j, SIB_OWN)
    start_own(opposite, FROM_Z2)
    send_weights(0)
    send_weights(1)
    get_basis.wait()
    get_act.wait()
    acc[...] = jnp.zeros_like(acc)
    accumulate(z)
    for k in range(nz - 1):
        zs = source(k)
        arrived(rows(zs, opposite, c), sem(FROM_Z2, zs))
        relay(rows(zs, opposite, c), zs, opposite, FROM_Z2, jnp.where(zs < z, z + 1, z - 1))
        to_sibling(zs, opposite, SIB_O)
        arrived(rows(zs, a, c), sem(FROM_A, zs))
        to_sibling(zs, a, SIB_A)
        arrived(rows(zs, b, c), sem(FROM_B, zs))
        to_sibling(zs, b, SIB_B)
        if k == nz - 2:
            forward_weights(0)
            forward_weights(1)
        if k >= 1:
            collect(source(k - 1))
            accumulate(source(k - 1))
    collect(source(nz - 2))
    accumulate(source(nz - 2))

    parts = 4
    rank = basis.shape[1] // parts

    def cols(p):
        return pl.ds(p * rank, rank)

    def low_rows(place, core, p):
        return low.at[place, pl.ds(pl.multiple_of(core * tokens, tokens), tokens), cols(p)]

    low[j, pl.ds(pl.multiple_of(c * tokens, tokens), tokens), :] = acc[...].astype(BF16)
    for p in range(parts):
        for n, target in enumerate((to_a, to_b, to_o, to_sib)):
            push(low_rows(j, c, p), low_rows(j, c, p), arrive_low.at[7 * p + n], target)
    put_basis = pltpu.make_async_copy(basis, basis_out, local.at[4])
    put_basis.start()
    for n, place in enumerate((a, b, opposite)):
        arrived(grads.at[place], arrive_grads.at[n])

    def part_ref(ref, peer, p):
        return ref.at[peer, :, cols(p)]

    for p in range(parts):
        for n, place in enumerate((a, b, opposite)):
            arrived(low_rows(place, c, p), arrive_low.at[7 * p + n])
            push(low_rows(place, c, p), low_rows(place, c, p), arrive_low.at[7 * p + 4 + n], to_sib)
        if p == 0:
            send_weights(2)
            send_weights(3)
        for n, place in ((3, j), (4, a), (5, b), (6, opposite)):
            arrived(low_rows(place, 1 - c, p), arrive_low.at[7 * p + n])
        total = jnp.dot(grads[0], low[0, :, cols(p)], preferred_element_type=F32)
        for place in range(1, 4):
            total += jnp.dot(grads[place], low[place, :, cols(p)], preferred_element_type=F32)
        sums[...] = total
        for zs in range(nz):
            part_out[zs, :, cols(p)] = sums[zs * owned : (zs + 1) * owned, :].astype(BF16)

        for peer in peers:
            push(part_ref(part_out, peer, p), part_ref(part_in, z, p), arrive_part.at[p * nz + z], {"dp": peer})
        part_own[:, cols(p)] = sums[pl.ds(pl.multiple_of(z * owned, owned), owned), :]
    forward_weights(2)
    get_first.wait()
    get_second.wait()

    for p in range(parts):
        at = cols(p)
        for peer in peers:
            arrived(part_ref(part_in, peer, p), arrive_part.at[p * nz + peer])
            part_own[:, at] += part_in[peer, :, at].astype(F32)
        projected = part_own[:, at]
        first_new = beta_one * first[:, at] + (1.0 - beta_one) * projected
        second_new = beta_two * second[:, at] + (1.0 - beta_two) * projected * projected
        first_out[:, at] = first_new
        second_out[:, at] = second_new
        corrected = first_new / (1.0 - beta_one**STEP)
        scaled = jnp.sqrt(second_new / (1.0 - beta_two**STEP)) + epsilon
        direction[j, :, at] = (corrected / scaled).astype(BF16)
        for n, target in enumerate((to_a, to_b, to_o)):
            push(direction.at[j, :, at], direction.at[j, :, at], arrive_dir.at[3 * p + n], target)
    forward_weights(3)
    for p in range(parts):
        for n, place in enumerate((a, b, opposite)):
            arrived(direction.at[place, :, cols(p)], arrive_dir.at[3 * p + n])
    put_direction = pltpu.make_async_copy(direction, direction_out, local.at[5])
    put_direction.start()
    for n in range(4):
        finish_weights(n)
    get_weights.wait()
    put_basis.wait()
    put_direction.wait()
    for copy in pending:
        copy.wait_send()
    for inside, copy in hops:
        pl.when(inside)(copy.wait_send)


def shards(nz, activations, out_grads, basis, weights, first_moment, second_moment):
    tokens, width = activations.shape
    shard, rank = basis.shape
    owned = first_moment.shape[1]
    features = 4 * owned
    vmem = pl.BlockSpec(memory_space=pltpu.VMEM)
    hbm = pl.BlockSpec(memory_space=pltpu.HBM)
    dma = pltpu.SemaphoreType.DMA
    parts = 4
    sends = (nz - 1) * 6 + 3 + 12 + parts * (nz - 1 + 7 + 3)
    gathered, weight_rows, direction, first_new, second_new = pl.pallas_call(
        functools.partial(kernel, nz),
        out_shape=(
            jax.ShapeDtypeStruct((nz * shard, rank), BF16),
            jax.ShapeDtypeStruct((4, owned, width), BF16),
            jax.ShapeDtypeStruct((4, owned, rank), BF16),
            jax.ShapeDtypeStruct((owned, rank), F32),
            jax.ShapeDtypeStruct((owned, rank), F32),
        ),
        in_specs=[hbm] * 6,
        out_specs=(hbm, hbm, hbm, vmem, vmem),
        scratch_shapes=[
            pltpu.VMEM((tokens // 2, width), BF16),
            pltpu.VMEM((nz * shard, rank), BF16),
            pltpu.VMEM((tokens, 4 * nz * owned), BF16),
            pltpu.VMEM((4, nz * owned, tokens), BF16),
            pltpu.VMEM((4, nz * owned, tokens), BF16),
            pltpu.VMEM((4, tokens, rank), BF16),
            pltpu.VMEM((nz, owned, rank), BF16),
            pltpu.VMEM((nz, owned, rank), BF16),
            pltpu.VMEM((owned, rank), F32),
            pltpu.VMEM((nz * owned, rank // parts), F32),
            pltpu.VMEM((4, owned, rank), BF16),
            pltpu.VMEM((tokens // 2, rank), F32),
            pltpu.VMEM((owned, rank), F32),
            pltpu.VMEM((owned, rank), F32),
            dma((8,)),
            dma((2 * (nz + 1),)),
            dma((sends,)),
            dma((8 * nz,)),
            dma((3,)),
            dma((parts * 7,)),
            dma((parts * nz,)),
            dma((parts * 3,)),
            dma((12,)),
        ],
        compiler_params=pltpu.CompilerParams(
            collective_id=0, has_side_effects=True, vmem_limit_bytes=60 * 2**20
        ),
        name="gather_and_step",
    )(activations, out_grads[:, 0, :], basis, weights[0], first_moment[0], second_moment[0])
    update = lax.dot_general(
        direction.reshape(features, rank), gathered, (((1,), (1,)), ((), ())),
        preferred_element_type=F32,
    )
    rows = weight_rows.reshape(features, width)
    new_weights = (rows.astype(F32) - step_scale * update).astype(BF16)
    return (new_weights[None], first_new[None], second_new[None])


def solution(mesh):
    return jax.shard_map(
        functools.partial(shards, mesh.shape["dp"]),
        mesh=mesh,
        in_specs=(
            P(("dp", "fsdp"), None),
            P(("dp", "fsdp"), "tensor", None),
            P("dp", None),
            P("tensor", ("dp", "fsdp"), None),
            P("tensor", ("dp", "fsdp"), None),
            P("tensor", ("dp", "fsdp"), None),
        ),
        out_specs=(
            P("tensor", "dp", None),
            P("tensor", ("dp", "fsdp"), None),
            P("tensor", ("dp", "fsdp"), None),
        ),
        check_vma=False,
    )
```
